256 devices in a mesh: fsdp: 32 (over x, y, core), tensor: 8 (over z).
Axes of the slice: x: 4, y: 4, z: 8, core: 2. Of those that a mesh axis runs over, the one named last changes fastest.
Arguments:
- momentum: float32 [8192, 28672], P('fsdp', 'tensor'), may hold values from -250 to 250
- gradient: bfloat16 [8192, 28672], P('fsdp', 'tensor'), may hold values from -3 to 3
- weight: bfloat16 [8192, 28672], P('fsdp', 'tensor'), may hold values from -6 to 6
- basis: float32 [28672, 256], P(('tensor', 'fsdp')), may hold values from -6 to 6
Outputs:
- new_momentum: float32 [8192, 28672], P('fsdp', 'tensor')
- new_weight: bfloat16 [8192, 28672], P('fsdp', 'tensor')
- new_basis: float32 [28672, 256], P(('tensor', 'fsdp'))
The draws below stay inside these ranges and needn't reach their ends.
All inputs are finite; a program needn't handle non-finite values.
Results may differ from the reference program's by a relative error of at most 0.001.
Values sent between devices are 32-bit elements; how exact they have to be, the bound alone decides.
No kernel may reach another device: no remote copies, remote signals or barrier semaphores. Data moves between devices by JAX's collectives and lax.ppermute only.
A program may use at most 64 MiB of HBM per device.

```python
import math
import jax
import jax.numpy as jnp
from jax import lax

D = 8192
FF = 28672
RANK = 256


def draw_momentum(key, part):
    key = jax.random.fold_in(key, 11)
    keys = jax.random.split(key, 3)
    row_pos = jnp.arange(D, dtype=jnp.float32) / (D - 1)
    col_pos = jnp.arange(FF, dtype=jnp.float32) / (FF - 1)
    row_scale = 10.0 ** (0.5 * jax.random.uniform(keys[0], (D,), jnp.float32) + 0.5 * row_pos)
    col_scale = 10.0 ** (0.5 * jax.random.uniform(keys[1], (FF,), jnp.float32) + 0.5 * col_pos)
    base = jnp.clip(jax.random.normal(keys[2], (D, FF), jnp.float32), -5.0, 5.0)
    return 0.1 * row_scale[:, None] * col_scale[None, :] * base


def steps_of(rng, dims, pieces, low, largest):
    gain = 1.0
    for axis_at, blocks in pieces:
        steps = jax.random.uniform(jax.random.fold_in(jax.random.fold_in(rng, 6), axis_at), (blocks,), jnp.float32, low / len(pieces), largest / len(pieces))
        gain = gain * jnp.repeat(jnp.exp(steps), dims[axis_at] // blocks).reshape((-1,) + (1,) * (len(dims) - 1 - axis_at))
    return gain


def centred(own_key, dims, deviation, bound, pieces=(), kind=jnp.bfloat16):
    gain = steps_of(own_key, dims, pieces, -0.22, 0.18) if pieces else 1.0
    entries = jax.random.normal(own_key, dims, jnp.float32) * deviation * gain
    return jnp.minimum(jnp.maximum(entries, -bound), bound).astype(kind)


def setup_inputs(seed: int = 0) -> dict:
    seeds = jax.random.split(jax.random.key(seed), 5)
    return {
        "momentum": draw_momentum(jax.random.fold_in(seeds[4], 71), 0),
        "gradient": centred(seeds[1], (D, FF), 0.5, 3.0, ((0, 32), (1, 8))),
        "weight": centred(seeds[2], (D, FF), 1.0, 6.0, ((0, 32), (1, 8))),
        "basis": centred(seeds[3], (FF, RANK), 1.0, 6.0, ((0, 256),), jnp.float32),
    }


keep_rate = 0.95
step_size = 0.25
decay_rate = 0.1

def reference(momentum, gradient, weight, basis):
    highest = lax.Precision.HIGHEST
    buffer = momentum + gradient.astype(jnp.float32)
    proj = jnp.dot(buffer, basis, precision=highest)
    gram = jnp.dot(proj.T, proj, precision=highest)
    lower = jnp.linalg.cholesky(gram)
    ortho = lax.linalg.triangular_solve(lower, proj, left_side=False, lower=True, transpose_a=True)
    back = jnp.dot(buffer.T, ortho, precision=highest)
    rms = jnp.sqrt(lax.optimization_barrier(jnp.mean(back * back, axis=0)) + 1e-06)
    new_basis = back / rms
    new_momentum = buffer - (1.0 - keep_rate) * jnp.dot(ortho, back.T, precision=highest)
    update = jnp.dot(ortho, new_basis.T, precision=highest)
    scale = step_size * math.sqrt(FF / D)
    new_weight = ((1.0 - step_size * decay_rate) * weight.astype(jnp.float32) - scale * update).astype(jnp.bfloat16)
    return (new_momentum, new_weight, new_basis)
```

```python
import math

import jax
import jax.numpy as jnp
from jax import lax
from jax.experimental import pallas as pl
from jax.experimental.pallas import tpu as pltpu
from jax.sharding import Mesh, PartitionSpec as P

keep_rate = 0.95
step_size = 0.25
decay_rate = 0.1

F32 = jnp.float32
BF16 = jnp.bfloat16
HIGH = lax.Precision.HIGH
HIGHEST = lax.Precision.HIGHEST
VMEM = pltpu.VMEM


def split(x):
    hi = x.astype(BF16)
    lo = (x - hi.astype(F32)).astype(BF16)
    return hi, lo


def nt(a, b):
    return lax.dot_general(a, b, (((1,), (1,)), ((), ())), preferred_element_type=F32)


def sort_columns_kernel(core_ref, mom_ref, grad_ref, keep_ref, send_ref, *, count):
    buffer = mom_ref[...] + grad_ref[...].astype(F32)
    chunks = buffer.shape[1] // count
    parts = [
        jnp.concatenate(
            [buffer[:, i * count : (i + 1) * count] for i in range(first, chunks, 2)], axis=1
        )
        for first in range(2)
    ]

    @pl.when(core_ref[0] == 0)
    def _():
        keep_ref[...] = parts[0]
        send_ref[...] = parts[1]

    @pl.when(core_ref[0] == 1)
    def _():
        keep_ref[...] = parts[1]
        send_ref[...] = parts[0]


def sort_columns(core, momentum, gradient, count):
    rows, cols = momentum.shape
    tile = 64
    spec = pl.BlockSpec((tile, cols), lambda i: (i, 0))
    half = pl.BlockSpec((tile, cols // 2), lambda i: (i, 0))
    out = jax.ShapeDtypeStruct((rows, cols // 2), F32)
    return pl.pallas_call(
        lambda *refs: sort_columns_kernel(*refs, count=count),
        grid=(rows // tile,),
        in_specs=[pl.BlockSpec(memory_space=pltpu.SMEM), spec, spec],
        out_specs=[half, half],
        out_shape=[out, out],
        compiler_params=pltpu.CompilerParams(vmem_limit_bytes=40 * 2**20),
        cost_estimate=pl.CostEstimate(flops=rows * cols, bytes_accessed=rows * cols * 10, transcendentals=0),
    )(core, momentum, gradient)


def bc(x):
    return jnp.broadcast_to(x, (8, 128))


def inverse_factor_kernel(g_ref, x_ref, a, w):
    n = g_ref.shape[0]
    a[...] = g_ref[...]
    w[...] = (
        lax.broadcasted_iota(jnp.int32, (n, n), 0) == lax.broadcasted_iota(jnp.int32, (n, n), 1)
    ).astype(F32)
    outer = 128
    for r0 in range(0, n, outer):
        tiles = [(a, t) for t in range(r0, n, 128)] + [(w, t) for t in range(0, r0 + outer, 128)]
        for s in range(outer // 8):
            top = r0 + 8 * s
            below = range(top + 8, r0 + outer, 8)
            cols = [[bc(a[i : i + 8, top + m : top + m + 1]) for m in range(8)] for i in below]
            own = [bc(a[top : top + 8, top + m : top + m + 1]) for m in range(8)]
            e = [[bc(own[j][i : i + 1, :]) if i >= j else None for j in range(8)] for i in range(8)]
            inv = [None] * 8
            for j in range(8):
                inv[j] = lax.rsqrt(e[j][j])
                for i in range(j + 1, 8):
                    e[i][j] = e[i][j] * inv[j]
                for k in range(j + 1, 8):
                    for i in range(k, 8):
                        e[i][k] = e[i][k] - e[i][j] * e[k][j]
            xs = [[None] * 8 for _ in range(8)]
            for i in range(8):
                xs[i][i] = inv[i]
                for j in range(i):
                    total = e[i][j] * xs[j][j]
                    for k in range(j + 1, i):
                        total = total + e[i][k] * xs[k][j]
                    xs[i][j] = -total * inv[i]
            for ref, t in tiles:
                rows = [bc(ref[top + k : top + k + 1, t : t + 128]) for k in range(8)]
                made = []
                for i in range(8):
                    total = xs[i][0] * rows[0]
                    for k in range(1, i + 1):
                        total = total + xs[i][k] * rows[k]
                    made.append(total)
                if len(below):
                    back = []
                    for m in range(8):
                        total = xs[m][m] * made[m]
                        for i in range(m + 1, 8):
                            total = total + xs[i][m] * made[i]
                        back.append(total)
                    for n_at, i in enumerate(below):
                        value = ref[i : i + 8, t : t + 128]
                        for m in range(8):
                            value = value - cols[n_at][m] * back[m]
                        ref[i : i + 8, t : t + 128] = value
                sub = lax.broadcasted_iota(jnp.int32, (8, 128), 0)
                row = made[0]
                for i in range(1, 8):
                    row = jnp.where(sub == i, made[i], row)
                ref[top : top + 8, t : t + 128] = row
        if r0 + outer < n:
            end = r0 + outer
            u = a[r0:end, end:n]
            for ref, lo, hi in ((a, end, n), (w, 0, end)):
                ref[end:n, lo:hi] -= lax.dot_general(
                    u, ref[r0:end, lo:hi], (((0,), (0,)), ((), ())),
                    precision=HIGHEST, preferred_element_type=F32,
                )
    x_ref[...] = w[...]


def inverse_factor(gram):
    n = gram.shape[0]
    return pl.pallas_call(
        inverse_factor_kernel,
        out_shape=jax.ShapeDtypeStruct((n, n), F32),
        in_specs=[pl.BlockSpec(memory_space=VMEM)],
        out_specs=pl.BlockSpec(memory_space=VMEM),
        scratch_shapes=[VMEM((n, n), F32), VMEM((n, n), F32)],
        compiler_params=pltpu.CompilerParams(vmem_limit_bytes=16 * 2**20),
        cost_estimate=pl.CostEstimate(flops=n**3, bytes_accessed=8 * n * n, transcendentals=0),
    )(gram)


def update_kernel(core_ref, mom_ref, grad_ref, weight_ref, m1_ref, m2_ref, own_ref, other_ref,
                  new_mom_ref, new_weight_ref, s_ref, *, count):
    pairs = s_ref.shape[0] // (2 * count)
    for i in range(pairs):
        first = pl.multiple_of((2 * i + core_ref[0]) * count, 8)
        second = pl.multiple_of((2 * i + 1 - core_ref[0]) * count, 8)
        s_ref[pl.ds(first, count), :] = own_ref[i]
        s_ref[pl.ds(second, count), :] = other_ref[i]
    s_hi, s_lo = split(s_ref[...])
    m2_hi, m2_lo = split(m2_ref[...])
    m1_hi = m1_ref[...].astype(BF16)
    buffer = mom_ref[...] + grad_ref[...].astype(F32)
    new_mom_ref[...] = buffer - nt(m1_hi, s_hi)
    update = nt(m2_hi, s_hi) + nt(m2_hi, s_lo) + nt(m2_lo, s_hi)
    new_weight_ref[...] = (
        (1.0 - step_size * decay_rate) * weight_ref[...].astype(F32) - update
    ).astype(BF16)


def updates(core, momentum, gradient, weight, m1, m2, own, other):
    rows, cols = momentum.shape
    chunks, count, rank = own.shape
    tiles = 4
    per = chunks // tiles
    spec = pl.BlockSpec((rows, cols // tiles), lambda i: (0, i))
    whole = pl.BlockSpec((rows, rank), lambda i: (0, 0))
    part = pl.BlockSpec((per, count, rank), lambda i: (i, 0, 0))
    return pl.pallas_call(
        lambda *refs: update_kernel(*refs, count=count),
        grid=(tiles,),
        in_specs=[pl.BlockSpec(memory_space=pltpu.SMEM), spec, spec, spec, whole, whole, part, part],
        out_specs=[spec, spec],
        out_shape=[jax.ShapeDtypeStruct((rows, cols), F32), jax.ShapeDtypeStruct((rows, cols), BF16)],
        scratch_shapes=[VMEM((2 * per * count, rank), F32)],
        compiler_params=pltpu.CompilerParams(vmem_limit_bytes=40 * 2**20),
        cost_estimate=pl.CostEstimate(
            flops=8 * rows * cols * rank, bytes_accessed=rows * cols * 16, transcendentals=0
        ),
    )(core, momentum, gradient, weight, m1, m2, own, other)


def tn(a, b):
    return lax.dot_general(a, b, (((0,), (0,)), ((), ())), precision=HIGH, preferred_element_type=F32)


def across_cores(x):
    return lax.ppermute(x, "c", [(0, 1), (1, 0)])


def gather(x, axes, n):
    spread = jnp.broadcast_to(x[None], (n,) + x.shape)
    return lax.all_to_all(spread, axes, 0, 0)


def per_device(momentum, gradient, weight, basis):
    chips = lax.axis_size("x") * lax.axis_size("y")
    cores = lax.axis_size("c")
    depth = lax.axis_size("z")
    plane = ("x", "y")
    rows, cols = momentum.shape
    count, rank = basis.shape
    total_cols = cols * depth
    total_rows = rows * chips * cores
    core = lax.axis_index("c").astype(jnp.int32).reshape(1)

    keep, send = sort_columns(core, momentum, gradient, count)
    recv = across_cores(send)
    right = gather(basis, plane, chips).reshape(chips * count, rank)

    mine = jnp.dot(keep, right, precision=HIGH)
    theirs = jnp.dot(recv, right, precision=HIGH)
    partial = mine + across_cores(theirs)
    share = rows // depth
    piece = jnp.sum(lax.all_to_all(partial.reshape(depth, share, rank), "z", 0, 0), axis=0)
    proj = gather(piece, "z", depth).reshape(rows, rank)
    proj_other = across_cores(proj)

    raw = tn(keep, proj) + tn(recv, proj_other)
    gram_part = tn(proj, proj) + tn(proj_other, proj_other)
    gram_share = rank // chips
    packed = jnp.concatenate(
        [raw.reshape(chips, count, rank), gram_part.reshape(chips, gram_share, rank)], axis=1
    )
    summed = jnp.sum(lax.all_to_all(packed, plane, 0, 0), axis=0)
    everything = gather(summed, plane, chips)
    half = everything[:, :count]
    gram = everything[:, count:].reshape(rank, rank)
    half_other = across_cores(half)

    inverse = inverse_factor(gram)
    back = lax.dot_general(
        half.reshape(chips * count, rank), inverse, (((1,), (1,)), ((), ())), precision=HIGH
    )
    sums = jnp.sum(back * back, axis=0)
    sums = jnp.sum(
        gather(jnp.broadcast_to(sums[None], (8, rank)), ("c", "z"), cores * depth), axis=0
    )[0]
    rms = jnp.sqrt(sums / total_cols + 1e-06)

    own_back = lax.dot_general(
        summed[:count], inverse, (((1,), (1,)), ((), ())), precision=HIGH
    )
    new_basis = own_back / rms
    ortho = lax.dot_general(proj, inverse, (((1,), (1,)), ((), ())), precision=HIGH)
    scale = step_size * math.sqrt(total_cols / total_rows)
    m1 = jnp.dot((1.0 - keep_rate) * ortho, inverse, precision=HIGH)
    m2 = jnp.dot(scale * ortho / rms, inverse, precision=HIGH)
    new_momentum, new_weight = updates(
        core, momentum, gradient, weight, m1, m2, half, half_other
    )
    return new_momentum, new_weight, new_basis


def solution(mesh):
    fsdp, depth = mesh.devices.shape
    grid = Mesh(mesh.devices.reshape(4, 4, 2, depth), ("x", "y", "c", "z"))
    block = P(("x", "y", "c"), "z")
    rows = P(("z", "x", "y", "c"), None)
    return jax.shard_map(
        per_device, mesh=grid, in_specs=(block, block, block, rows),
        out_specs=(block, block, rows), check_vma=False,
    )
```

```python
import functools
import math

import jax
import jax.numpy as jnp
from jax import lax
from jax.experimental import pallas as pl
from jax.experimental.pallas import tpu as pltpu
from jax.sharding import Mesh, PartitionSpec as P

keep_rate = 0.95
step_size = 0.25
decay_rate = 0.1

F32 = jnp.float32
BF16 = jnp.bfloat16
HIGH = lax.Precision.HIGH
HIGHEST = lax.Precision.HIGHEST
VMEM = pltpu.VMEM


def split(x):
    hi = x.astype(BF16)
    lo = (x - hi.astype(F32)).astype(BF16)
    return hi, lo


def nt(a, b):
    return lax.dot_general(a, b, (((1,), (1,)), ((), ())), preferred_element_type=F32)


def sort_columns_kernel(core_ref, mom_ref, grad_ref, keep_ref, send_ref, mom, grad, sems, *, count):
    steps, tile, cols = mom.shape
    loads = []
    for t in range(steps):
        rows = pl.ds(t * tile, tile)
        pair = (
            pltpu.make_async_copy(mom_ref.at[rows, :], mom.at[t], sems.at[0, t]),
            pltpu.make_async_copy(grad_ref.at[rows, :], grad.at[t], sems.at[1, t]),
        )
        for load in pair:
            load.start()
        loads.append(pair)
    for t in range(steps):
        for load in loads[t]:
            load.wait()
        buffer = mom[t] + grad[t].astype(F32)
        parts = [
            jnp.concatenate(
                [buffer[:, i * count : (i + 1) * count] for i in range(first, cols // count, 2)],
                axis=1,
            )
            for first in range(2)
        ]
        rows = pl.ds(t * tile, tile)

        @pl.when(core_ref[0] == 0)
        def _():
            keep_ref[rows, :] = parts[0]
            send_ref[rows, :] = parts[1]

        @pl.when(core_ref[0] == 1)
        def _():
            keep_ref[rows, :] = parts[1]
            send_ref[rows, :] = parts[0]


def sort_columns(core, momentum, gradient, count):
    rows, cols = momentum.shape
    steps = 8
    out = jax.ShapeDtypeStruct((rows, cols // 2), F32)
    hbm = pl.BlockSpec(memory_space=pltpu.HBM)
    vmem = pl.BlockSpec(memory_space=VMEM)
    return pl.pallas_call(
        lambda *refs: sort_columns_kernel(*refs, count=count),
        in_specs=[pl.BlockSpec(memory_space=pltpu.SMEM), hbm, hbm],
        out_specs=[vmem, vmem],
        out_shape=[out, out],
        scratch_shapes=[
            VMEM((steps, rows // steps, cols), F32),
            VMEM((steps, rows // steps, cols), BF16),
            pltpu.SemaphoreType.DMA((2, steps)),
        ],
        compiler_params=pltpu.CompilerParams(vmem_limit_bytes=53 * 2**20),
        cost_estimate=pl.CostEstimate(flops=rows * cols, bytes_accessed=rows * cols * 10, transcendentals=0),
    )(core, momentum, gradient)


def bc(x):
    return jnp.broadcast_to(x, (8, 128))


def dot3(dims, a, b):
    a_hi, a_lo = split(a)
    b_hi, b_lo = split(b)
    dot = functools.partial(
        lax.dot_general, dimension_numbers=(dims, ((), ())), preferred_element_type=F32
    )
    return dot(a_hi, b_hi) + dot(a_hi, b_lo) + dot(a_lo, b_hi)


NT = ((1,), (1,))
NN = ((1,), (0,))


def factor_kernel(got_ref, proj_ref, own_ref, x_ref, ortho_ref, m1_ref, back_ref, sums_ref, a, w):
    chips, packed, n = got_ref.shape
    count, share = own_ref.shape[0], n // chips
    for i in range(chips):
        a[i * share : (i + 1) * share, :] = got_ref[i, count:, :]
    w[...] = (
        lax.broadcasted_iota(jnp.int32, (n, n), 0) == lax.broadcasted_iota(jnp.int32, (n, n), 1)
    ).astype(F32)
    outer = 128
    for r0 in range(0, n, outer):
        tiles = [(a, t) for t in range(r0, n, 128)] + [(w, t) for t in range(0, r0 + outer, 128)]
        for s in range(outer // 8):
            top = r0 + 8 * s
            below = range(top + 8, r0 + outer, 8)
            cols = [[bc(a[i : i + 8, top + m : top + m + 1]) for m in range(8)] for i in below]
            own = [bc(a[top : top + 8, top + m : top + m + 1]) for m in range(8)]
            e = [[bc(own[j][i : i + 1, :]) if i >= j else None for j in range(8)] for i in range(8)]
            inv = [None] * 8
            for j in range(8):
                inv[j] = lax.rsqrt(e[j][j])
                for i in range(j + 1, 8):
                    e[i][j] = e[i][j] * inv[j]
                for k in range(j + 1, 8):
                    for i in range(k, 8):
                        e[i][k] = e[i][k] - e[i][j] * e[k][j]
            xs = [[None] * 8 for _ in range(8)]
            for i in range(8):
                xs[i][i] = inv[i]
                for j in range(i):
                    total = e[i][j] * xs[j][j]
                    for k in range(j + 1, i):
                        total = total + e[i][k] * xs[k][j]
                    xs[i][j] = -total * inv[i]
            for ref, t in tiles:
                rows = [bc(ref[top + k : top + k + 1, t : t + 128]) for k in range(8)]
                made = []
                for i in range(8):
                    total = xs[i][0] * rows[0]
                    for k in range(1, i + 1):
                        total = total + xs[i][k] * rows[k]
                    made.append(total)
                if len(below):
                    back = []
                    for m in range(8):
                        total = xs[m][m] * made[m]
                        for i in range(m + 1, 8):
                            total = total + xs[i][m] * made[i]
                        back.append(total)
                    for n_at, i in enumerate(below):
                        value = ref[i : i + 8, t : t + 128]
                        for m in range(8):
                            value = value - cols[n_at][m] * back[m]
                        ref[i : i + 8, t : t + 128] = value
                sub = lax.broadcasted_iota(jnp.int32, (8, 128), 0)
                row = made[0]
                for i in range(1, 8):
                    row = jnp.where(sub == i, made[i], row)
                ref[top : top + 8, t : t + 128] = row
        if r0 + outer < n:
            end = r0 + outer
            u = a[r0:end, end:n]
            for ref, lo, hi in ((a, end, n), (w, 0, end)):
                ref[end:n, lo:hi] -= lax.dot_general(
                    u, ref[r0:end, lo:hi], (((0,), (0,)), ((), ())),
                    precision=HIGHEST, preferred_element_type=F32,
                )
    inverse = w[...]
    x_ref[...] = inverse
    total = jnp.zeros((1, n), F32)
    for i in range(0, chips, 4):
        rows = jnp.concatenate([got_ref[i + k, :count, :] for k in range(4)], axis=0)
        back = dot3(NT, rows, inverse)
        total = total + jnp.sum(back * back, axis=0, keepdims=True)
    sums_ref[...] = jnp.broadcast_to(total[None], sums_ref.shape)
    ortho = dot3(NT, proj_ref[...], inverse)
    ortho_ref[...] = ortho
    m1_ref[...] = dot3(NN, (1.0 - keep_rate) * ortho, inverse)
    back_ref[...] = dot3(NT, own_ref[...], inverse)


def factor(got, proj, own, copies):
    n = got.shape[2]
    rows = proj.shape[0]
    vmem = pl.BlockSpec(memory_space=VMEM)
    return pl.pallas_call(
        factor_kernel,
        out_shape=[
            jax.ShapeDtypeStruct((n, n), F32),
            jax.ShapeDtypeStruct((rows, n), F32),
            jax.ShapeDtypeStruct((rows, n), F32),
            jax.ShapeDtypeStruct(own.shape, F32),
            jax.ShapeDtypeStruct((copies, 8, n), F32),
        ],
        in_specs=[vmem] * 3,
        out_specs=[vmem] * 5,
        scratch_shapes=[VMEM((n, n), F32), VMEM((n, n), F32)],
        compiler_params=pltpu.CompilerParams(vmem_limit_bytes=16 * 2**20),
        cost_estimate=pl.CostEstimate(flops=40 * n**3, bytes_accessed=16 * n * n, transcendentals=0),
    )(got, proj, own)


TILES = 4
HBM = pl.BlockSpec(memory_space=pltpu.HBM)
IN_VMEM = pl.BlockSpec(memory_space=VMEM)
IN_SMEM = pl.BlockSpec(memory_space=pltpu.SMEM)


def copies_of(pairs, sems):
    return [pltpu.make_async_copy(src, dst, sems.at[i]) for i, (src, dst) in enumerate(pairs)]


def momentum_kernel(core_ref, mom_ref, grad_ref, m1_ref, own_ref, other_ref,
                    out_ref, hi_ref, lo_ref,
                    mom, grad, own, other, out, hi, lo, load_sems, store_sems):
    tiles, rows, width = mom.shape
    chunks, count, _ = own.shape
    per = chunks // tiles
    loads, stores = [], []
    for t in range(tiles):
        cols, part = pl.ds(t * width, width), pl.ds(t * per, per)
        loads.append(copies_of(
            [
                (own_ref.at[part], own.at[part]), (other_ref.at[part], other.at[part]),
                (mom_ref.at[:, cols], mom.at[t]), (grad_ref.at[:, cols], grad.at[t]),
            ],
            load_sems.at[t],
        ))
        stores.append(copies_of(
            [
                (hi.at[cols], hi_ref.at[cols]), (lo.at[cols], lo_ref.at[cols]),
                (out.at[t], out_ref.at[:, cols]),
            ],
            store_sems.at[t],
        ))
        for load in loads[t]:
            load.start()
    m1 = m1_ref[...].astype(BF16)
    for t in range(tiles):
        loads[t][0].wait()
        loads[t][1].wait()
        for i in range(t * per, (t + 1) * per):
            mine = pl.ds(pl.multiple_of((2 * i + core_ref[0]) * count, 16), count)
            theirs = pl.ds(pl.multiple_of((2 * i + 1 - core_ref[0]) * count, 16), count)
            hi[mine, :], lo[mine, :] = split(own[i])
            hi[theirs, :], lo[theirs, :] = split(other[i])
        stores[t][0].start()
        stores[t][1].start()
        change = nt(m1, hi[t * width : (t + 1) * width, :])
        loads[t][2].wait()
        loads[t][3].wait()
        out[t] = mom[t] + grad[t].astype(F32) - change
        stores[t][2].start()
    for group in stores:
        for store in group:
            store.wait()


def update_momentum(core, momentum, gradient, m1, own, other):
    rows, cols = momentum.shape
    rank = own.shape[2]
    factor_part = jax.ShapeDtypeStruct((cols, rank), BF16)
    tile = (TILES, rows, cols // TILES)
    return pl.pallas_call(
        momentum_kernel,
        in_specs=[IN_SMEM, HBM, HBM, IN_VMEM, HBM, HBM],
        out_specs=[HBM] * 3,
        out_shape=[jax.ShapeDtypeStruct((rows, cols), F32), factor_part, factor_part],
        scratch_shapes=[
            VMEM(tile, F32), VMEM(tile, BF16), VMEM(own.shape, F32), VMEM(own.shape, F32),
            VMEM(tile, F32), VMEM((cols, rank), BF16), VMEM((cols, rank), BF16),
            pltpu.SemaphoreType.DMA((TILES, 4)), pltpu.SemaphoreType.DMA((TILES, 3)),
        ],
        compiler_params=pltpu.CompilerParams(vmem_limit_bytes=53 * 2**20),
        cost_estimate=pl.CostEstimate(
            flops=2 * rows * cols * rank, bytes_accessed=rows * cols * 18, transcendentals=0
        ),
    )(core, momentum, gradient, m1, own, other)


def weight_kernel(weight_ref, got_ref, ortho_ref, x_ref, back_ref, hi_ref, lo_ref,
                  out_ref, basis_ref,
                  weight, hi, lo, out, load_sems, store_sems, *, scale, total_cols):
    tiles, rows, width = out.shape
    loads, stores = [], []
    for t in range(tiles):
        cols = pl.ds(t * width, width)
        loads.append(copies_of(
            [
                (hi_ref.at[cols], hi.at[cols]), (lo_ref.at[cols], lo.at[cols]),
                (weight_ref.at[:, cols], weight.at[t]),
            ],
            load_sems.at[t],
        ))
        stores.append(
            pltpu.make_async_copy(out.at[t], out_ref.at[:, cols], store_sems.at[t])
        )
        for load in loads[t]:
            load.start()
    sums = got_ref[0, 0:1, :]
    for i in range(1, got_ref.shape[0]):
        sums = sums + got_ref[i, 0:1, :]
    rms = jnp.sqrt(sums / total_cols + 1e-06)
    basis_ref[...] = back_ref[...] / rms
    left_hi, left_lo = split(dot3(NN, scale * ortho_ref[...] / rms, x_ref[...]))
    for t in range(tiles):
        for load in loads[t]:
            load.wait()
        right_hi = hi[t * width : (t + 1) * width, :]
        right_lo = lo[t * width : (t + 1) * width, :]
        change = nt(left_hi, right_hi) + nt(left_hi, right_lo) + nt(left_lo, right_hi)
        out[t] = (
            (1.0 - step_size * decay_rate) * weight[t].astype(F32) - change
        ).astype(BF16)
        stores[t].start()
    for store in stores:
        store.wait()


def update_weight(weight, got, ortho, inverse, back, hi, lo, scale, total_cols):
    rows, cols = weight.shape
    count, rank = back.shape
    tile = (TILES, rows, cols // TILES)
    return pl.pallas_call(
        functools.partial(weight_kernel, scale=scale, total_cols=total_cols),
        in_specs=[HBM] + [IN_VMEM] * 4 + [HBM] * 2,
        out_specs=[HBM, IN_VMEM],
        out_shape=[
            jax.ShapeDtypeStruct((rows, cols), BF16), jax.ShapeDtypeStruct((count, rank), F32)
        ],
        scratch_shapes=[
            VMEM(tile, BF16), VMEM((cols, rank), BF16), VMEM((cols, rank), BF16),
            VMEM(tile, BF16),
            pltpu.SemaphoreType.DMA((TILES, 3)), pltpu.SemaphoreType.DMA((TILES,)),
        ],
        compiler_params=pltpu.CompilerParams(vmem_limit_bytes=53 * 2**20),
        cost_estimate=pl.CostEstimate(
            flops=6 * rows * cols * rank, bytes_accessed=rows * cols * 8, transcendentals=0
        ),
    )(weight, got, ortho, inverse, back, hi, lo)


def tn(a, b):
    return lax.dot_general(a, b, (((0,), (0,)), ((), ())), precision=HIGH, preferred_element_type=F32)


def across_cores(x):
    return lax.ppermute(x, "c", [(0, 1), (1, 0)])


def gather(x, axes, n):
    spread = jnp.broadcast_to(x[None], (n,) + x.shape)
    return lax.all_to_all(spread, axes, 0, 0)


def per_device(momentum, gradient, weight, basis):
    chips = lax.axis_size("x") * lax.axis_size("y")
    cores = lax.axis_size("c")
    depth = lax.axis_size("z")
    plane = ("x", "y")
    rows, cols = momentum.shape
    count, rank = basis.shape
    total_cols = cols * depth
    total_rows = rows * chips * cores
    core = lax.axis_index("c").astype(jnp.int32).reshape(1)

    keep, send = sort_columns(core, momentum, gradient, count)
    recv = across_cores(send)
    right = gather(basis, plane, chips).reshape(chips * count, rank)

    mine = jnp.dot(keep, right, precision=HIGH)
    theirs = jnp.dot(recv, right, precision=HIGH)
    partial = mine + across_cores(theirs)
    share = rows // depth
    piece = jnp.sum(lax.all_to_all(partial.reshape(depth, share, rank), "z", 0, 0), axis=0)
    proj = gather(piece, "z", depth).reshape(rows, rank)
    proj_other = across_cores(proj)

    raw = tn(keep, proj) + tn(recv, proj_other)
    gram_part = tn(proj, proj) + tn(proj_other, proj_other)
    gram_share = rank // chips
    packed = jnp.concatenate(
        [raw.reshape(chips, count, rank), gram_part.reshape(chips, gram_share, rank)], axis=1
    )
    summed = jnp.sum(lax.all_to_all(packed, plane, 0, 0), axis=0)
    everything = gather(summed, plane, chips)
    half = everything[:, :count]
    half_other = across_cores(half)
    inverse, ortho, m1, back, sums = factor(everything, proj, summed[:count], cores * depth)
    sums = lax.all_to_all(sums, ("c", "z"), 0, 0)
    new_momentum, hi, lo = update_momentum(core, momentum, gradient, m1, half, half_other)
    sums, hi, lo = lax.optimization_barrier((sums, hi, lo))
    scale = step_size * math.sqrt(total_cols / total_rows)
    new_weight, new_basis = update_weight(
        weight, sums, ortho, inverse, back, hi, lo, scale, total_cols
    )
    return new_momentum, new_weight, new_basis


def solution(mesh):
    fsdp, depth = mesh.devices.shape
    grid = Mesh(mesh.devices.reshape(4, 4, 2, depth), ("x", "y", "c", "z"))
    block = P(("x", "y", "c"), "z")
    rows = P(("z", "x", "y", "c"), None)
    return jax.shard_map(
        per_device, mesh=grid, in_specs=(block, block, block, rows),
        out_specs=(block, block, rows), check_vma=False,
    )
```

```python
import functools
import math

import jax
import jax.numpy as jnp
from jax import lax
from jax.experimental import pallas as pl
from jax.experimental.pallas import tpu as pltpu
from jax.sharding import Mesh, PartitionSpec as P

keep_rate = 0.95
step_size = 0.25
decay_rate = 0.1

F32 = jnp.float32
BF16 = jnp.bfloat16
HIGH = lax.Precision.HIGH
HIGHEST = lax.Precision.HIGHEST
VMEM = pltpu.VMEM
TILES = 4
HBM = pl.BlockSpec(memory_space=pltpu.HBM)
IN_VMEM = pl.BlockSpec(memory_space=VMEM)
IN_SMEM = pl.BlockSpec(memory_space=pltpu.SMEM)


def split(x):
    hi = x.astype(BF16)
    lo = (x - hi.astype(F32)).astype(BF16)
    return hi, lo


def nt(a, b):
    return lax.dot_general(a, b, (((1,), (1,)), ((), ())), preferred_element_type=F32)


def copies_of(pairs, sems):
    return [pltpu.make_async_copy(src, dst, sems.at[i]) for i, (src, dst) in enumerate(pairs)]


def sort_columns_kernel(core_ref, mom_ref, grad_ref, keep_ref, send_ref,
                        mom, grad, keep, send, load_sems, store_sems, *, count):
    steps, tile, cols = mom.shape
    loads, stores = [], []
    for t in range(steps):
        rows = pl.ds(t * tile, tile)
        loads.append(copies_of(
            [(mom_ref.at[rows, :], mom.at[t]), (grad_ref.at[rows, :], grad.at[t])],
            load_sems.at[t],
        ))
        stores.append(copies_of(
            [(send.at[t], send_ref.at[rows, :]), (keep.at[t], keep_ref.at[rows, :])],
            store_sems.at[t],
        ))
        for load in loads[t]:
            load.start()
    for t in range(steps):
        for load in loads[t]:
            load.wait()
        buffer = mom[t] + grad[t].astype(F32)
        parts = [
            jnp.concatenate(
                [buffer[:, i * count : (i + 1) * count] for i in range(first, cols // count, 2)],
                axis=1,
            )
            for first in range(2)
        ]

        @pl.when(core_ref[0] == 0)
        def _():
            keep[t] = parts[0]
            send[t] = parts[1]

        @pl.when(core_ref[0] == 1)
        def _():
            keep[t] = parts[1]
            send[t] = parts[0]

        for store in stores[t]:
            store.start()
    for group in stores:
        for store in group:
            store.wait()


def sort_columns(core, momentum, gradient, count):
    rows, cols = momentum.shape
    steps = 8
    tile = rows // steps
    out = jax.ShapeDtypeStruct((rows, cols // 2), F32)
    return pl.pallas_call(
        lambda *refs: sort_columns_kernel(*refs, count=count),
        in_specs=[IN_SMEM, HBM, HBM],
        out_specs=[HBM, HBM],
        out_shape=[out, out],
        scratch_shapes=[
            VMEM((steps, tile, cols), F32), VMEM((steps, tile, cols), BF16),
            VMEM((steps, tile, cols // 2), F32), VMEM((steps, tile, cols // 2), F32),
            pltpu.SemaphoreType.DMA((steps, 2)), pltpu.SemaphoreType.DMA((steps, 2)),
        ],
        compiler_params=pltpu.CompilerParams(vmem_limit_bytes=53 * 2**20),
        cost_estimate=pl.CostEstimate(
            flops=rows * cols, bytes_accessed=rows * cols * 10, transcendentals=0
        ),
    )(core, momentum, gradient)


def bc(x):
    return jnp.broadcast_to(x, (8, 128))


def split3(x):
    hi = x.astype(BF16)
    rest = x - hi.astype(F32)
    mid = rest.astype(BF16)
    return hi, mid, (rest - mid.astype(F32)).astype(BF16)


def dot3(dims, a, b):
    a_hi, a_lo = split(a)
    b_hi, b_lo = split(b)
    dot = functools.partial(
        lax.dot_general, dimension_numbers=(dims, ((), ())), preferred_element_type=F32
    )
    return dot(a_hi, b_hi) + dot(a_hi, b_lo) + dot(a_lo, b_hi)


NT = ((1,), (1,))


def eliminate(top, below, tiles, a):
    cols = [[bc(a[i : i + 8, top + m : top + m + 1]) for m in range(8)] for i in below]
    own = [bc(a[top : top + 8, top + m : top + m + 1]) for m in range(8)]
    e = [[bc(own[j][i : i + 1, :]) if i >= j else None for j in range(8)] for i in range(8)]
    inv = [None] * 8
    for j in range(8):
        inv[j] = lax.rsqrt(e[j][j])
        for i in range(j + 1, 8):
            e[i][j] = e[i][j] * inv[j]
        for k in range(j + 1, 8):
            for i in range(k, 8):
                e[i][k] = e[i][k] - e[i][j] * e[k][j]
    xs = [[None] * 8 for _ in range(8)]
    for i in range(8):
        xs[i][i] = inv[i]
        for j in range(i):
            total = e[i][j] * xs[j][j]
            for k in range(j + 1, i):
                total = total + e[i][k] * xs[k][j]
            xs[i][j] = -total * inv[i]
    sub = lax.broadcasted_iota(jnp.int32, (8, 128), 0)
    for ref, t in tiles:
        rows = [bc(ref[top + k : top + k + 1, t : t + 128]) for k in range(8)]
        made = []
        for i in range(8):
            total = xs[i][0] * rows[0]
            for k in range(1, i + 1):
                total = total + xs[i][k] * rows[k]
            made.append(total)
        if below:
            back = []
            for m in range(8):
                total = xs[m][m] * made[m]
                for i in range(m + 1, 8):
                    total = total + xs[i][m] * made[i]
                back.append(total)
            for n_at, i in enumerate(below):
                value = ref[i : i + 8, t : t + 128]
                for m in range(8):
                    value = value - cols[n_at][m] * back[m]
                ref[i : i + 8, t : t + 128] = value
        row = made[0]
        for i in range(1, 8):
            row = jnp.where(sub == i, made[i], row)
        ref[top : top + 8, t : t + 128] = row


def factor_kernel(got_ref, proj_ref, back_ref, ortho_ref, sums_ref, a, w):
    chips, packed, n = got_ref.shape
    share = n // chips
    count = packed - share
    panel = 32
    for i in range(chips):
        a[i * share : (i + 1) * share, :] = got_ref[i, count:, :]
    w[...] = (
        lax.broadcasted_iota(jnp.int32, (n, n), 0) == lax.broadcasted_iota(jnp.int32, (n, n), 1)
    ).astype(F32)
    for r0 in range(0, n, panel):
        end = r0 + panel
        tiles = [(a, t) for t in range(r0 // 128 * 128, n, 128)]
        tiles += [(w, t) for t in range(0, end, 128)]
        for top in range(r0, end, 8):
            eliminate(top, list(range(top + 8, end, 8)), tiles, a)
        if end < n:
            lo, width = end // 128 * 128, -(-end // 128) * 128
            u = a[r0:end, lo:]
            v = jnp.concatenate([u, w[r0:end, :width]], axis=1)
            uh, um, ul = split3(u)
            vh, vm, vl = split3(v)
            change = lax.dot_general(
                jnp.concatenate([uh, uh, um, uh, ul, um], axis=0),
                jnp.concatenate([vh, vm, vh, vl, vh, vm], axis=0),
                (((0,), (0,)), ((), ())), preferred_element_type=F32,
            )
            a[end:n, lo:] -= change[end - lo :, : n - lo]
            w[end:n, :width] -= change[end - lo :, n - lo :]
    inverse = w[...]
    total = jnp.zeros((1, n), F32)
    group = 4
    for i in range(0, chips, group):
        rows = jnp.concatenate([got_ref[i + k, :count, :] for k in range(group)], axis=0)
        back = dot3(NT, rows, inverse)
        for k in range(group):
            back_ref[i + k] = back[k * count : (k + 1) * count]
        total = total + jnp.sum(back * back, axis=0, keepdims=True)
    sums_ref[...] = jnp.broadcast_to(total[None], sums_ref.shape)
    ortho_ref[...] = dot3(NT, proj_ref[...], inverse)


def factor(got, proj, copies):
    chips, packed, n = got.shape
    rows = proj.shape[0]
    return pl.pallas_call(
        factor_kernel,
        out_shape=[
            jax.ShapeDtypeStruct((chips, packed - n // chips, n), F32),
            jax.ShapeDtypeStruct((rows, n), F32),
            jax.ShapeDtypeStruct((copies, 8, n), F32),
        ],
        in_specs=[IN_VMEM] * 2,
        out_specs=[IN_VMEM] * 3,
        scratch_shapes=[VMEM((n, n), F32), VMEM((n, n), F32)],
        compiler_params=pltpu.CompilerParams(vmem_limit_bytes=16 * 2**20),
        cost_estimate=pl.CostEstimate(flops=40 * n**3, bytes_accessed=16 * n * n, transcendentals=0),
    )(got, proj)


def place(core, count, per, own, other, hi, lo, t):
    for i in range(t * per, (t + 1) * per):
        mine = pl.ds(pl.multiple_of((2 * i + core) * count, 16), count)
        theirs = pl.ds(pl.multiple_of((2 * i + 1 - core) * count, 16), count)
        for rows, value in ((mine, own[i]), (theirs, other[i])):
            hi[rows, :] = value.astype(BF16)
            if lo is not None:
                lo[rows, :] = (value - value.astype(BF16).astype(F32)).astype(BF16)


def early_kernel(core_ref, mom_ref, grad_ref, ortho_ref, own_ref, other_ref, out_ref,
                 mom, grad, own, other, out, hi, load_sems, store_sems):
    tiles, rows, width = mom.shape
    chunks, count, _ = own.shape
    per = chunks // tiles
    loads, stores = [], []
    for t in range(tiles):
        cols, part = pl.ds(t * width, width), pl.ds(t * per, per)
        loads.append(copies_of(
            [
                (own_ref.at[part], own.at[part]), (other_ref.at[part], other.at[part]),
                (mom_ref.at[:, cols], mom.at[t]), (grad_ref.at[:, cols], grad.at[t]),
            ],
            load_sems.at[t],
        ))
        stores.append(pltpu.make_async_copy(out.at[t], out_ref.at[:, cols], store_sems.at[t]))
        for load in loads[t]:
            load.start()
    left = ((1.0 - keep_rate) * ortho_ref[...]).astype(BF16)
    for t in range(tiles):
        for load in loads[t]:
            load.wait()
        place(core_ref[0], count, per, own, other, hi, None, t)
        change = nt(left, hi[t * width : (t + 1) * width, :])
        out[t] = mom[t] + grad[t].astype(F32) - change
        stores[t].start()
    for store in stores:
        store.wait()


def update_early(core, momentum, gradient, ortho, own, other, tiles):
    rows, cols = momentum.shape
    chunks, count, rank = own.shape
    width = cols // TILES
    tile = (tiles, rows, width)
    part = (chunks // TILES * tiles, count, rank)
    return pl.pallas_call(
        early_kernel,
        in_specs=[IN_SMEM, HBM, HBM, IN_VMEM, HBM, HBM],
        out_specs=HBM,
        out_shape=jax.ShapeDtypeStruct((rows, cols), F32),
        scratch_shapes=[
            VMEM(tile, F32), VMEM(tile, BF16), VMEM(part, F32), VMEM(part, F32),
            VMEM(tile, F32), VMEM((tiles * width, rank), BF16),
            pltpu.SemaphoreType.DMA((tiles, 4)), pltpu.SemaphoreType.DMA((tiles,)),
        ],
        compiler_params=pltpu.CompilerParams(vmem_limit_bytes=53 * 2**20),
        cost_estimate=pl.CostEstimate(
            flops=2 * rows * cols * rank, bytes_accessed=rows * cols * 18, transcendentals=0
        ),
    )(core, momentum, gradient, ortho, own, other)


def late_kernel(place_ref, mom_ref, grad_ref, weight_ref, got_ref, ortho_ref, own_ref, other_ref,
                begun_ref, new_mom_ref, new_weight_ref, basis_ref,
                mom, grad, weight, own, other, new_mom, new_weight, hi, lo,
                load_sems, store_sems, *, early, scale, total_cols):
    tiles, rows, width = weight.shape
    chunks, count, _ = own.shape
    per = chunks // tiles
    loads, stores = [], []
    order = list(range(early, tiles)) + list(range(early))
    for t in order:
        cols, part = pl.ds(t * width, width), pl.ds(t * per, per)
        pairs = [
            (own_ref.at[part], own.at[part]), (other_ref.at[part], other.at[part]),
            (weight_ref.at[:, cols], weight.at[t]),
        ]
        results = [(new_weight.at[t], new_weight_ref.at[:, cols])]
        if t >= early:
            pairs += [
                (mom_ref.at[:, cols], mom.at[t - early]),
                (grad_ref.at[:, cols], grad.at[t - early]),
            ]
            results.append((new_mom.at[t - early], new_mom_ref.at[:, cols]))
        loads.append(copies_of(pairs, load_sems.at[t]))
        stores.append(copies_of(results, store_sems.at[t]))
        for load in loads[-1]:
            load.start()
    sums = got_ref[0, 0:1, :]
    for i in range(1, got_ref.shape[0]):
        sums = sums + got_ref[i, 0:1, :]
    rms = jnp.sqrt(sums / total_cols + 1e-06)
    ortho = ortho_ref[...]
    first = ((1.0 - keep_rate) * ortho).astype(BF16)
    left_hi, left_lo = split(scale * ortho / rms)
    for t, load_group, store_group in zip(order, loads, stores):
        for load in load_group:
            load.wait()
        place(place_ref[0], count, per, own, other, hi, lo, t)
        right_hi = hi[t * width : (t + 1) * width, :]
        right_lo = lo[t * width : (t + 1) * width, :]
        if t >= early:
            new_mom[t - early] = (
                mom[t - early] + grad[t - early].astype(F32) - nt(first, right_hi)
            )
        change = nt(left_hi, right_hi) + nt(left_hi, right_lo) + nt(left_lo, right_hi)
        new_weight[t] = (
            (1.0 - step_size * decay_rate) * weight[t].astype(F32) - change
        ).astype(BF16)
        for store in store_group:
            store.start()
    basis_ref[...] = own[place_ref[1]] / rms
    for group in stores:
        for store in group:
            store.wait()


def update_late(where, momentum, gradient, weight, got, ortho, own, other, begun, early, scale,
                total_cols):
    rows, cols = weight.shape
    chunks, count, rank = own.shape
    tile = (TILES, rows, cols // TILES)
    rest = (TILES - early, rows, cols // TILES)
    return pl.pallas_call(
        functools.partial(late_kernel, early=early, scale=scale, total_cols=total_cols),
        in_specs=[IN_SMEM, HBM, HBM, HBM, IN_VMEM, IN_VMEM, HBM, HBM, HBM],
        out_specs=[HBM, HBM, IN_VMEM],
        out_shape=[
            jax.ShapeDtypeStruct((rows, cols), F32), jax.ShapeDtypeStruct((rows, cols), BF16),
            jax.ShapeDtypeStruct((count, rank), F32),
        ],
        scratch_shapes=[
            VMEM(rest, F32), VMEM(rest, BF16), VMEM(tile, BF16),
            VMEM(own.shape, F32), VMEM(own.shape, F32), VMEM(rest, F32), VMEM(tile, BF16),
            VMEM((cols, rank), BF16), VMEM((cols, rank), BF16),
            pltpu.SemaphoreType.DMA((TILES, 5)), pltpu.SemaphoreType.DMA((TILES, 2)),
        ],
        input_output_aliases={8: 0},
        compiler_params=pltpu.CompilerParams(vmem_limit_bytes=53 * 2**20),
        cost_estimate=pl.CostEstimate(
            flops=8 * rows * cols * rank, bytes_accessed=rows * cols * 18, transcendentals=0
        ),
    )(where, momentum, gradient, weight, got, ortho, own, other, begun)


def tn(a, b):
    return lax.dot_general(a, b, (((0,), (0,)), ((), ())), precision=HIGH, preferred_element_type=F32)


def across_cores(x):
    return lax.ppermute(x, "c", [(0, 1), (1, 0)])


def gather(x, axes, n):
    spread = jnp.broadcast_to(x[None], (n,) + x.shape)
    return lax.all_to_all(spread, axes, 0, 0)


def per_device(momentum, gradient, weight, basis):
    chips = lax.axis_size("x") * lax.axis_size("y")
    cores = lax.axis_size("c")
    depth = lax.axis_size("z")
    plane = ("x", "y")
    rows, cols = momentum.shape
    count, rank = basis.shape
    total_cols = cols * depth
    total_rows = rows * chips * cores
    core = lax.axis_index("c").astype(jnp.int32).reshape(1)

    keep, send = sort_columns(core, momentum, gradient, count)
    recv = across_cores(send)
    right = gather(basis, plane, chips).reshape(chips * count, rank)

    mine = jnp.dot(keep, right, precision=HIGH)
    theirs = jnp.dot(recv, right, precision=HIGH)
    partial = mine + across_cores(theirs)
    share = rows // depth
    piece = jnp.sum(lax.all_to_all(partial.reshape(depth, share, rank), "z", 0, 0), axis=0)
    proj = gather(piece, "z", depth).reshape(rows, rank)
    proj_other = across_cores(proj)

    raw = tn(keep, proj) + tn(recv, proj_other)
    gram_part = tn(proj, proj) + tn(proj_other, proj_other)
    gram_share = rank // chips
    packed = jnp.concatenate(
        [raw.reshape(chips, count, rank), gram_part.reshape(chips, gram_share, rank)], axis=1
    )
    summed = jnp.sum(lax.all_to_all(packed, plane, 0, 0), axis=0)
    everything = gather(summed, plane, chips)
    back, ortho, sums = factor(everything, proj, cores * depth)
    back_other = across_cores(back)
    sums = lax.all_to_all(sums, ("c", "z"), 0, 0)
    early = 2
    begun = update_early(core, momentum, gradient, ortho, back, back_other, early)
    sums, begun = lax.optimization_barrier((sums, begun))
    chip = (lax.axis_index("x") * lax.axis_size("y") + lax.axis_index("y")).astype(jnp.int32)
    where = jnp.concatenate([core, chip.reshape(1)])
    scale = step_size * math.sqrt(total_cols / total_rows)
    new_momentum, new_weight, new_basis = update_late(
        where, momentum, gradient, weight, sums, ortho, back, back_other, begun, early, scale,
        total_cols,
    )
    return new_momentum, new_weight, new_basis


def solution(mesh):
    fsdp, depth = mesh.devices.shape
    grid = Mesh(mesh.devices.reshape(4, 4, 2, depth), ("x", "y", "c", "z"))
    block = P(("x", "y", "c"), "z")
    rows = P(("z", "x", "y", "c"), None)
    return jax.shard_map(
        per_device, mesh=grid, in_specs=(block, block, block, rows),
        out_specs=(block, block, rows), check_vma=False,
    )
```

```python
import functools
import math

import jax
import jax.numpy as jnp
from jax import lax
from jax.experimental import pallas as pl
from jax.experimental.pallas import tpu as pltpu
from jax.sharding import Mesh, PartitionSpec as P

keep_rate = 0.95
step_size = 0.25
decay_rate = 0.1

F32 = jnp.float32
BF16 = jnp.bfloat16
HIGH = lax.Precision.HIGH
HIGHEST = lax.Precision.HIGHEST
VMEM = pltpu.VMEM
TILES = 4
HBM = pl.BlockSpec(memory_space=pltpu.HBM)
IN_VMEM = pl.BlockSpec(memory_space=VMEM)
IN_SMEM = pl.BlockSpec(memory_space=pltpu.SMEM)


def split(x):
    hi = x.astype(BF16)
    lo = (x - hi.astype(F32)).astype(BF16)
    return hi, lo


def nt(a, b):
    return lax.dot_general(a, b, (((1,), (1,)), ((), ())), preferred_element_type=F32)


def nn(a, b):
    return lax.dot_general(a, b, (((1,), (0,)), ((), ())), preferred_element_type=F32)


def copies_of(pairs, sems):
    return [pltpu.make_async_copy(src, dst, sems.at[i]) for i, (src, dst) in enumerate(pairs)]


def sort_columns_kernel(core_ref, mom_ref, grad_ref, keep_ref, send_ref,
                        mom, grad, keep, send, load_sems, store_sems, *, count):
    steps, tile, cols = mom.shape
    loads, stores = [], []
    for t in range(steps):
        rows = pl.ds(t * tile, tile)
        loads.append(copies_of(
            [(mom_ref.at[rows, :], mom.at[t]), (grad_ref.at[rows, :], grad.at[t])],
            load_sems.at[t],
        ))
        stores.append(copies_of(
            [(send.at[t], send_ref.at[rows, :]), (keep.at[t], keep_ref.at[rows, :])],
            store_sems.at[t],
        ))
        for load in loads[t]:
            load.start()
    for t in range(steps):
        for load in loads[t]:
            load.wait()
        buffer = mom[t] + grad[t].astype(F32)
        parts = [
            jnp.concatenate(
                [buffer[:, i * count : (i + 1) * count] for i in range(first, cols // count, 2)],
                axis=1,
            )
            for first in range(2)
        ]

        @pl.when(core_ref[0] == 0)
        def _():
            keep[t] = parts[0]
            send[t] = parts[1]

        @pl.when(core_ref[0] == 1)
        def _():
            keep[t] = parts[1]
            send[t] = parts[0]

        for store in stores[t]:
            store.start()
    for group in stores:
        for store in group:
            store.wait()


def sort_columns(core, momentum, gradient, count):
    rows, cols = momentum.shape
    steps = 8
    tile = rows // steps
    out = jax.ShapeDtypeStruct((rows, cols // 2), F32)
    return pl.pallas_call(
        lambda *refs: sort_columns_kernel(*refs, count=count),
        in_specs=[IN_SMEM, HBM, HBM],
        out_specs=[HBM, HBM],
        out_shape=[out, out],
        scratch_shapes=[
            VMEM((steps, tile, cols), F32), VMEM((steps, tile, cols), BF16),
            VMEM((steps, tile, cols // 2), F32), VMEM((steps, tile, cols // 2), F32),
            pltpu.SemaphoreType.DMA((steps, 2)), pltpu.SemaphoreType.DMA((steps, 2)),
        ],
        compiler_params=pltpu.CompilerParams(vmem_limit_bytes=53 * 2**20),
        cost_estimate=pl.CostEstimate(
            flops=rows * cols, bytes_accessed=rows * cols * 10, transcendentals=0
        ),
    )(core, momentum, gradient)


def bc(x):
    return jnp.broadcast_to(x, (8, 128))


def split3(x):
    hi = x.astype(BF16)
    rest = x - hi.astype(F32)
    mid = rest.astype(BF16)
    return hi, mid, (rest - mid.astype(F32)).astype(BF16)


def dot3(dims, a, b):
    a_hi, a_lo = split(a)
    b_hi, b_lo = split(b)
    dot = functools.partial(
        lax.dot_general, dimension_numbers=(dims, ((), ())), preferred_element_type=F32
    )
    return dot(a_hi, b_hi) + dot(a_hi, b_lo) + dot(a_lo, b_hi)


NT = ((1,), (1,))


def eliminate(top, below, tiles, a):
    cols = [[bc(a[i : i + 8, top + m : top + m + 1]) for m in range(8)] for i in below]
    own = [bc(a[top : top + 8, top + m : top + m + 1]) for m in range(8)]
    e = [[bc(own[j][i : i + 1, :]) if i >= j else None for j in range(8)] for i in range(8)]
    inv = [None] * 8
    for j in range(8):
        inv[j] = lax.rsqrt(e[j][j])
        for i in range(j + 1, 8):
            e[i][j] = e[i][j] * inv[j]
        for k in range(j + 1, 8):
            for i in range(k, 8):
                e[i][k] = e[i][k] - e[i][j] * e[k][j]
    xs = [[None] * 8 for _ in range(8)]
    for i in range(8):
        xs[i][i] = inv[i]
        for j in range(i):
            total = e[i][j] * xs[j][j]
            for k in range(j + 1, i):
                total = total + e[i][k] * xs[k][j]
            xs[i][j] = -total * inv[i]
    sub = lax.broadcasted_iota(jnp.int32, (8, 128), 0)
    for ref, t in tiles:
        rows = [bc(ref[top + k : top + k + 1, t : t + 128]) for k in range(8)]
        made = []
        for i in range(8):
            total = xs[i][0] * rows[0]
            for k in range(1, i + 1):
                total = total + xs[i][k] * rows[k]
            made.append(total)
        if below:
            back = []
            for m in range(8):
                total = xs[m][m] * made[m]
                for i in range(m + 1, 8):
                    total = total + xs[i][m] * made[i]
                back.append(total)
            for n_at, i in enumerate(below):
                value = ref[i : i + 8, t : t + 128]
                for m in range(8):
                    value = value - cols[n_at][m] * back[m]
                ref[i : i + 8, t : t + 128] = value
        row = made[0]
        for i in range(1, 8):
            row = jnp.where(sub == i, made[i], row)
        ref[top : top + 8, t : t + 128] = row


def factor_kernel(got_ref, proj_ref, back_ref, ortho_ref, sums_ref, a, w):
    chips, packed, n = got_ref.shape
    share = n // chips
    count = packed - share
    panel = 32
    for i in range(chips):
        a[i * share : (i + 1) * share, :] = got_ref[i, count:, :]
    w[...] = (
        lax.broadcasted_iota(jnp.int32, (n, n), 0) == lax.broadcasted_iota(jnp.int32, (n, n), 1)
    ).astype(F32)
    for r0 in range(0, n, panel):
        end = r0 + panel
        tiles = [(a, t) for t in range(r0 // 128 * 128, n, 128)]
        tiles += [(w, t) for t in range(0, end, 128)]
        for top in range(r0, end, 8):
            eliminate(top, list(range(top + 8, end, 8)), tiles, a)
        if end < n:
            lo, width = end // 128 * 128, -(-end // 128) * 128
            u = a[r0:end, lo:]
            v = jnp.concatenate([u, w[r0:end, :width]], axis=1)
            uh, um, ul = split3(u)
            vh, vm, vl = split3(v)
            change = lax.dot_general(
                jnp.concatenate([uh, uh, um, uh, ul, um], axis=0),
                jnp.concatenate([vh, vm, vh, vl, vh, vm], axis=0),
                (((0,), (0,)), ((), ())), preferred_element_type=F32,
            )
            a[end:n, lo:] -= change[end - lo :, : n - lo]
            w[end:n, :width] -= change[end - lo :, n - lo :]
    inverse = w[...]
    total = jnp.zeros((1, n), F32)
    group = 4
    for i in range(0, chips, group):
        rows = jnp.concatenate([got_ref[i + k, :count, :] for k in range(group)], axis=0)
        back = dot3(NT, rows, inverse)
        for k in range(group):
            back_ref[i + k] = back[k * count : (k + 1) * count]
        total = total + jnp.sum(back * back, axis=0, keepdims=True)
    sums_ref[...] = jnp.broadcast_to(total[None], sums_ref.shape)
    ortho_ref[...] = dot3(NT, proj_ref[...], inverse)


def factor(got, proj, copies):
    chips, packed, n = got.shape
    rows = proj.shape[0]
    return pl.pallas_call(
        factor_kernel,
        out_shape=[
            jax.ShapeDtypeStruct((chips, packed - n // chips, n), F32),
            jax.ShapeDtypeStruct((rows, n), F32),
            jax.ShapeDtypeStruct((copies, 8, n), F32),
        ],
        in_specs=[IN_VMEM] * 2,
        out_specs=[IN_VMEM] * 3,
        scratch_shapes=[VMEM((n, n), F32), VMEM((n, n), F32)],
        compiler_params=pltpu.CompilerParams(vmem_limit_bytes=16 * 2**20),
        cost_estimate=pl.CostEstimate(flops=40 * n**3, bytes_accessed=16 * n * n, transcendentals=0),
    )(got, proj)


def place(core, count, per, own, other, hi, lo, t):
    for i in range(t * per, (t + 1) * per):
        mine = pl.ds(pl.multiple_of((2 * i + core) * count, 16), count)
        theirs = pl.ds(pl.multiple_of((2 * i + 1 - core) * count, 16), count)
        for rows, value in ((mine, own[i]), (theirs, other[i])):
            hi[rows, :] = value.astype(BF16)
            if lo is not None:
                lo[rows, :] = (value - value.astype(BF16).astype(F32)).astype(BF16)


def early_kernel(core_ref, mom_ref, grad_ref, ortho_ref, own_ref, other_ref, out_ref,
                 mom, grad, own, other, out, hi, load_sems, store_sems):
    tiles, rows, width = mom.shape
    chunks, count, _ = own.shape
    per = chunks // tiles
    loads, stores = [], []
    for t in range(tiles):
        cols, part = pl.ds(t * width, width), pl.ds(t * per, per)
        loads.append(copies_of(
            [
                (own_ref.at[part], own.at[part]), (other_ref.at[part], other.at[part]),
                (mom_ref.at[:, cols], mom.at[t]), (grad_ref.at[:, cols], grad.at[t]),
            ],
            load_sems.at[t],
        ))
        stores.append(pltpu.make_async_copy(out.at[t], out_ref.at[:, cols], store_sems.at[t]))
        for load in loads[t]:
            load.start()
    left = ((1.0 - keep_rate) * ortho_ref[...]).astype(BF16)
    for t in range(tiles):
        for load in loads[t]:
            load.wait()
        place(core_ref[0], count, per, own, other, hi, None, t)
        change = nt(left, hi[t * width : (t + 1) * width, :])
        out[t] = mom[t] + grad[t].astype(F32) - change
        stores[t].start()
    for store in stores:
        store.wait()


def update_early(core, momentum, gradient, ortho, own, other, tiles):
    rows, cols = momentum.shape
    chunks, count, rank = own.shape
    width = cols // TILES
    tile = (tiles, rows, width)
    part = (chunks // TILES * tiles, count, rank)
    return pl.pallas_call(
        early_kernel,
        in_specs=[IN_SMEM, HBM, HBM, IN_VMEM, HBM, HBM],
        out_specs=HBM,
        out_shape=jax.ShapeDtypeStruct((rows, cols), F32),
        scratch_shapes=[
            VMEM(tile, F32), VMEM(tile, BF16), VMEM(part, F32), VMEM(part, F32),
            VMEM(tile, F32), VMEM((tiles * width, rank), BF16),
            pltpu.SemaphoreType.DMA((tiles, 4)), pltpu.SemaphoreType.DMA((tiles,)),
        ],
        compiler_params=pltpu.CompilerParams(vmem_limit_bytes=53 * 2**20),
        cost_estimate=pl.CostEstimate(
            flops=2 * rows * cols * rank, bytes_accessed=rows * cols * 18, transcendentals=0
        ),
    )(core, momentum, gradient, ortho, own, other)


def late_kernel(place_ref, mom_ref, grad_ref, weight_ref, got_ref, ortho_ref, own_ref, other_ref,
                begun_ref, new_mom_ref, new_weight_ref, basis_ref,
                mom, grad, weight, own, other, new_mom, new_weight, hi, lo,
                load_sems, store_sems, *, early, scale, total_cols):
    tiles, rows, width = weight.shape
    chunks, count, _ = own.shape
    per = chunks // tiles
    loads, stores = [], []
    order = list(range(early, tiles)) + list(range(early))
    for t in order:
        cols, part = pl.ds(t * width, width), pl.ds(t * per, per)
        pairs = [
            (own_ref.at[part], own.at[part]), (other_ref.at[part], other.at[part]),
            (weight_ref.at[:, cols], weight.at[t]),
        ]
        results = [(new_weight.at[t], new_weight_ref.at[:, cols])]
        if t >= early:
            pairs += [
                (mom_ref.at[:, cols], mom.at[t - early]),
                (grad_ref.at[:, cols], grad.at[t - early]),
            ]
            results.append((new_mom.at[t - early], new_mom_ref.at[:, cols]))
        loads.append(copies_of(pairs, load_sems.at[t]))
        stores.append(copies_of(results, store_sems.at[t]))
        for load in loads[-1]:
            load.start()
    sums = got_ref[0, 0:1, :]
    for i in range(1, got_ref.shape[0]):
        sums = sums + got_ref[i, 0:1, :]
    rms = jnp.sqrt(sums / total_cols + 1e-06)
    ortho = ortho_ref[...]
    first = ((1.0 - keep_rate) * ortho).astype(BF16)
    left_hi, left_lo = split(scale * ortho / rms)
    for t, load_group, store_group in zip(order, loads, stores):
        for load in load_group:
            load.wait()
        place(place_ref[0], count, per, own, other, hi, lo, t)
        right_hi = hi[t * width : (t + 1) * width, :]
        right_lo = lo[t * width : (t + 1) * width, :]
        if t >= early:
            new_mom[t - early] = (
                mom[t - early] + grad[t - early].astype(F32) - nt(first, right_hi)
            )
        change = nt(left_hi, right_hi) + nt(left_hi, right_lo) + nt(left_lo, right_hi)
        new_weight[t] = (
            (1.0 - step_size * decay_rate) * weight[t].astype(F32) - change
        ).astype(BF16)
        for store in store_group:
            store.start()
    basis_ref[...] = own[place_ref[1]] / rms
    for group in stores:
        for store in group:
            store.wait()


def update_late(where, momentum, gradient, weight, got, ortho, own, other, begun, early, scale,
                total_cols):
    rows, cols = weight.shape
    chunks, count, rank = own.shape
    tile = (TILES, rows, cols // TILES)
    rest = (max(TILES - early, 1), rows, cols // TILES)
    return pl.pallas_call(
        functools.partial(late_kernel, early=early, scale=scale, total_cols=total_cols),
        in_specs=[IN_SMEM, HBM, HBM, HBM, IN_VMEM, IN_VMEM, HBM, HBM, HBM],
        out_specs=[HBM, HBM, IN_VMEM],
        out_shape=[
            jax.ShapeDtypeStruct((rows, cols), F32), jax.ShapeDtypeStruct((rows, cols), BF16),
            jax.ShapeDtypeStruct((count, rank), F32),
        ],
        scratch_shapes=[
            VMEM(rest, F32), VMEM(rest, BF16), VMEM(tile, BF16),
            VMEM(own.shape, F32), VMEM(own.shape, F32), VMEM(rest, F32), VMEM(tile, BF16),
            VMEM((cols, rank), BF16), VMEM((cols, rank), BF16),
            pltpu.SemaphoreType.DMA((TILES, 5)), pltpu.SemaphoreType.DMA((TILES, 2)),
        ],
        input_output_aliases={8: 0},
        compiler_params=pltpu.CompilerParams(vmem_limit_bytes=53 * 2**20),
        cost_estimate=pl.CostEstimate(
            flops=8 * rows * cols * rank, bytes_accessed=rows * cols * 18, transcendentals=0
        ),
    )(where, momentum, gradient, weight, got, ortho, own, other, begun)


def project_back_kernel(keep_ref, recv_ref, proj_ref, other_ref, out_ref):
    chips, packed, rank = out_ref.shape
    share = rank // chips
    count = packed - share
    proj = jnp.concatenate([proj_ref[...], other_ref[...]], axis=0)
    left_hi, left_lo = split(proj.T)
    per = 8
    width = per * count

    def product(right):
        hi, lo = split(right)
        return nn(left_hi, hi) + nn(left_hi, lo) + nn(left_lo, hi)

    gram = product(proj)
    for i in range(chips):
        out_ref[i, count:, :] = gram[i * share : (i + 1) * share, :]
    for t in range(chips // per):
        cols = slice(t * width, (t + 1) * width)
        raw = product(jnp.concatenate([keep_ref[:, cols], recv_ref[:, cols]], axis=0)).T
        for i in range(per):
            out_ref[t * per + i, :count, :] = raw[i * count : (i + 1) * count, :]


def project_back(keep, recv, proj, other, chips):
    rows, cols = keep.shape
    rank = proj.shape[1]
    return pl.pallas_call(
        project_back_kernel,
        in_specs=[IN_VMEM] * 4,
        out_specs=IN_VMEM,
        out_shape=jax.ShapeDtypeStruct((chips, cols // chips + rank // chips, rank), F32),
        compiler_params=pltpu.CompilerParams(vmem_limit_bytes=24 * 2**20),
        cost_estimate=pl.CostEstimate(
            flops=12 * rows * cols * rank, bytes_accessed=rows * cols * 8, transcendentals=0
        ),
    )(keep, recv, proj, other)


def across_cores(x):
    return lax.ppermute(x, "c", [(0, 1), (1, 0)])


def gather(x, axes, n):
    spread = jnp.broadcast_to(x[None], (n,) + x.shape)
    return lax.all_to_all(spread, axes, 0, 0)


def per_device(momentum, gradient, weight, basis):
    chips = lax.axis_size("x") * lax.axis_size("y")
    cores = lax.axis_size("c")
    depth = lax.axis_size("z")
    plane = ("x", "y")
    rows, cols = momentum.shape
    count, rank = basis.shape
    total_cols = cols * depth
    total_rows = rows * chips * cores
    core = lax.axis_index("c").astype(jnp.int32).reshape(1)

    keep, send = sort_columns(core, momentum, gradient, count)
    pieces = 4
    recv = jnp.concatenate([across_cores(piece) for piece in jnp.split(send, pieces, axis=0)])
    right = gather(basis, plane, chips).reshape(chips * count, rank)

    mine = jnp.dot(keep, right, precision=HIGH)
    theirs = jnp.dot(recv, right, precision=HIGH)
    partial = mine + across_cores(theirs)
    share = rows // depth
    piece = jnp.sum(lax.all_to_all(partial.reshape(depth, share, rank), "z", 0, 0), axis=0)
    proj = gather(piece, "z", depth).reshape(rows, rank)
    proj_other = across_cores(proj)

    packed = project_back(keep, recv, proj, proj_other, chips)
    summed = jnp.sum(lax.all_to_all(packed, plane, 0, 0), axis=0)
    everything = gather(summed, plane, chips)
    back, ortho, sums = factor(everything, proj, cores * depth)
    back_other = across_cores(back)
    sums = lax.all_to_all(sums, ("c", "z"), 0, 0)
    early = TILES
    begun = update_early(core, momentum, gradient, ortho, back, back_other, early)
    sums, begun = lax.optimization_barrier((sums, begun))
    chip = (lax.axis_index("x") * lax.axis_size("y") + lax.axis_index("y")).astype(jnp.int32)
    where = jnp.concatenate([core, chip.reshape(1)])
    scale = step_size * math.sqrt(total_cols / total_rows)
    new_momentum, new_weight, new_basis = update_late(
        where, momentum, gradient, weight, sums, ortho, back, back_other, begun, early, scale,
        total_cols,
    )
    return new_momentum, new_weight, new_basis


def solution(mesh):
    fsdp, depth = mesh.devices.shape
    grid = Mesh(mesh.devices.reshape(4, 4, 2, depth), ("x", "y", "c", "z"))
    block = P(("x", "y", "c"), "z")
    rows = P(("z", "x", "y", "c"), None)
    return jax.shard_map(
        per_device, mesh=grid, in_specs=(block, block, block, rows),
        out_specs=(block, block, rows), check_vma=False,
    )
```

```python
import functools
import math

import jax
import jax.numpy as jnp
from jax import lax
from jax.experimental import pallas as pl
from jax.experimental.pallas import tpu as pltpu
from jax.sharding import Mesh, PartitionSpec as P

keep_rate = 0.95
step_size = 0.25
decay_rate = 0.1

F32 = jnp.float32
BF16 = jnp.bfloat16
HIGH = lax.Precision.HIGH
HIGHEST = lax.Precision.HIGHEST
VMEM = pltpu.VMEM
TILES = 4
HBM = pl.BlockSpec(memory_space=pltpu.HBM)
IN_VMEM = pl.BlockSpec(memory_space=VMEM)
IN_SMEM = pl.BlockSpec(memory_space=pltpu.SMEM)


def split(x):
    hi = x.astype(BF16)
    lo = (x - hi.astype(F32)).astype(BF16)
    return hi, lo


def nt(a, b):
    return lax.dot_general(a, b, (((1,), (1,)), ((), ())), preferred_element_type=F32)


def nn(a, b):
    return lax.dot_general(a, b, (((1,), (0,)), ((), ())), preferred_element_type=F32)


def copies_of(pairs, sems):
    return [pltpu.make_async_copy(src, dst, sems.at[i]) for i, (src, dst) in enumerate(pairs)]


def sort_columns_kernel(core_ref, mom_ref, grad_ref, keep_ref, send_ref,
                        mom, grad, keep, send, load_sems, store_sems, *, count):
    steps, tile, cols = mom.shape
    loads, stores = [], []
    for t in range(steps):
        rows = pl.ds(t * tile, tile)
        loads.append(copies_of(
            [(mom_ref.at[rows, :], mom.at[t]), (grad_ref.at[rows, :], grad.at[t])],
            load_sems.at[t],
        ))
        stores.append(copies_of(
            [(send.at[t], send_ref.at[rows, :]), (keep.at[t], keep_ref.at[rows, :])],
            store_sems.at[t],
        ))
        for load in loads[t]:
            load.start()
    for t in range(steps):
        for load in loads[t]:
            load.wait()
        buffer = mom[t] + grad[t].astype(F32)
        parts = [
            jnp.concatenate(
                [buffer[:, i * count : (i + 1) * count] for i in range(first, cols // count, 2)],
                axis=1,
            )
            for first in range(2)
        ]

        @pl.when(core_ref[0] == 0)
        def _():
            keep[t] = parts[0]
            send[t] = parts[1]

        @pl.when(core_ref[0] == 1)
        def _():
            keep[t] = parts[1]
            send[t] = parts[0]

        for store in stores[t]:
            store.start()
    for group in stores:
        for store in group:
            store.wait()


def sort_columns(core, momentum, gradient, count):
    rows, cols = momentum.shape
    steps = 8
    tile = rows // steps
    out = jax.ShapeDtypeStruct((rows, cols // 2), F32)
    return pl.pallas_call(
        lambda *refs: sort_columns_kernel(*refs, count=count),
        in_specs=[IN_SMEM, HBM, HBM],
        out_specs=[HBM, HBM],
        out_shape=[out, out],
        scratch_shapes=[
            VMEM((steps, tile, cols), F32), VMEM((steps, tile, cols), BF16),
            VMEM((steps, tile, cols // 2), F32), VMEM((steps, tile, cols // 2), F32),
            pltpu.SemaphoreType.DMA((steps, 2)), pltpu.SemaphoreType.DMA((steps, 2)),
        ],
        compiler_params=pltpu.CompilerParams(vmem_limit_bytes=53 * 2**20),
        cost_estimate=pl.CostEstimate(
            flops=rows * cols, bytes_accessed=rows * cols * 10, transcendentals=0
        ),
    )(core, momentum, gradient)


def bc(x):
    return jnp.broadcast_to(x, (8, 128))


def split3(x):
    hi = x.astype(BF16)
    rest = x - hi.astype(F32)
    mid = rest.astype(BF16)
    return hi, mid, (rest - mid.astype(F32)).astype(BF16)


def dot3(dims, a, b):
    a_hi, a_lo = split(a)
    b_hi, b_lo = split(b)
    dot = functools.partial(
        lax.dot_general, dimension_numbers=(dims, ((), ())), preferred_element_type=F32
    )
    return dot(a_hi, b_hi) + dot(a_hi, b_lo) + dot(a_lo, b_hi)


NT = ((1,), (1,))


def eliminate(top, below, tiles, a):
    cols = [[bc(a[i : i + 8, top + m : top + m + 1]) for m in range(8)] for i in below]
    own = [bc(a[top : top + 8, top + m : top + m + 1]) for m in range(8)]
    e = [[bc(own[j][i : i + 1, :]) if i >= j else None for j in range(8)] for i in range(8)]
    inv = [None] * 8
    for j in range(8):
        inv[j] = lax.rsqrt(e[j][j])
        for i in range(j + 1, 8):
            e[i][j] = e[i][j] * inv[j]
        for k in range(j + 1, 8):
            for i in range(k, 8):
                e[i][k] = e[i][k] - e[i][j] * e[k][j]
    xs = [[None] * 8 for _ in range(8)]
    for i in range(8):
        xs[i][i] = inv[i]
        for j in range(i):
            total = e[i][j] * xs[j][j]
            for k in range(j + 1, i):
                total = total + e[i][k] * xs[k][j]
            xs[i][j] = -total * inv[i]
    sub = lax.broadcasted_iota(jnp.int32, (8, 128), 0)
    for ref, t in tiles:
        rows = [bc(ref[top + k : top + k + 1, t : t + 128]) for k in range(8)]
        made = []
        for i in range(8):
            total = xs[i][0] * rows[0]
            for k in range(1, i + 1):
                total = total + xs[i][k] * rows[k]
            made.append(total)
        if below:
            back = []
            for m in range(8):
                total = xs[m][m] * made[m]
                for i in range(m + 1, 8):
                    total = total + xs[i][m] * made[i]
                back.append(total)
            for n_at, i in enumerate(below):
                value = ref[i : i + 8, t : t + 128]
                for m in range(8):
                    value = value - cols[n_at][m] * back[m]
                ref[i : i + 8, t : t + 128] = value
        row = made[0]
        for i in range(1, 8):
            row = jnp.where(sub == i, made[i], row)
        ref[top : top + 8, t : t + 128] = row


def factor_kernel(got_ref, proj_ref, back_ref, ortho_ref, sums_ref, a, w):
    chips, packed, n = got_ref.shape
    share = n // chips
    count = packed - share
    panel = 32
    for i in range(chips):
        a[i * share : (i + 1) * share, :] = got_ref[i, count:, :]
    w[...] = (
        lax.broadcasted_iota(jnp.int32, (n, n), 0) == lax.broadcasted_iota(jnp.int32, (n, n), 1)
    ).astype(F32)
    for r0 in range(0, n, panel):
        end = r0 + panel
        tiles = [(a, t) for t in range(r0 // 128 * 128, n, 128)]
        tiles += [(w, t) for t in range(0, end, 128)]
        for top in range(r0, end, 8):
            eliminate(top, list(range(top + 8, end, 8)), tiles, a)
        if end < n:
            lo, width = end // 128 * 128, -(-end // 128) * 128
            u = a[r0:end, lo:]
            v = jnp.concatenate([u, w[r0:end, :width]], axis=1)
            uh, um, ul = split3(u)
            vh, vm, vl = split3(v)
            change = lax.dot_general(
                jnp.concatenate([uh, uh, um, uh, ul, um], axis=0),
                jnp.concatenate([vh, vm, vh, vl, vh, vm], axis=0),
                (((0,), (0,)), ((), ())), preferred_element_type=F32,
            )
            a[end:n, lo:] -= change[end - lo :, : n - lo]
            w[end:n, :width] -= change[end - lo :, n - lo :]
    inverse = w[...]
    total = jnp.zeros((1, n), F32)
    group = 4
    for i in range(0, chips, group):
        rows = jnp.concatenate([got_ref[i + k, :count, :] for k in range(group)], axis=0)
        back = dot3(NT, rows, inverse)
        for k in range(group):
            back_ref[i + k] = back[k * count : (k + 1) * count]
        total = total + jnp.sum(back * back, axis=0, keepdims=True)
    sums_ref[...] = jnp.broadcast_to(total[None], sums_ref.shape)
    ortho_ref[...] = dot3(NT, proj_ref[...], inverse)


def factor(got, proj, copies):
    chips, packed, n = got.shape
    rows = proj.shape[0]
    return pl.pallas_call(
        factor_kernel,
        out_shape=[
            jax.ShapeDtypeStruct((chips, packed - n // chips, n), F32),
            jax.ShapeDtypeStruct((rows, n), F32),
            jax.ShapeDtypeStruct((copies, 8, n), F32),
        ],
        in_specs=[IN_VMEM] * 2,
        out_specs=[IN_VMEM] * 3,
        scratch_shapes=[VMEM((n, n), F32), VMEM((n, n), F32)],
        compiler_params=pltpu.CompilerParams(vmem_limit_bytes=16 * 2**20),
        cost_estimate=pl.CostEstimate(flops=40 * n**3, bytes_accessed=16 * n * n, transcendentals=0),
    )(got, proj)


def place(core, count, per, own, other, hi, lo, t):
    for i in range(t * per, (t + 1) * per):
        mine = pl.ds(pl.multiple_of((2 * i + core) * count, 16), count)
        theirs = pl.ds(pl.multiple_of((2 * i + 1 - core) * count, 16), count)
        for rows, value in ((mine, own[i]), (theirs, other[i])):
            hi[rows, :], lo[rows, :] = split(value)


def early_kernel(core_ref, mom_ref, grad_ref, ortho_ref, own_ref, other_ref,
                 out_ref, hi_ref, lo_ref,
                 mom, grad, own, other, out, hi, lo, load_sems, store_sems):
    tiles, rows, width = mom.shape
    chunks, count, _ = own.shape
    per = chunks // tiles
    loads, stores = [], []
    for t in range(tiles):
        cols, part = pl.ds(t * width, width), pl.ds(t * per, per)
        loads.append(copies_of(
            [
                (own_ref.at[part], own.at[part]), (other_ref.at[part], other.at[part]),
                (mom_ref.at[:, cols], mom.at[t]), (grad_ref.at[:, cols], grad.at[t]),
            ],
            load_sems.at[t],
        ))
        stores.append(copies_of(
            [
                (hi.at[cols], hi_ref.at[cols]), (lo.at[cols], lo_ref.at[cols]),
                (out.at[t], out_ref.at[:, cols]),
            ],
            store_sems.at[t],
        ))
        for load in loads[t]:
            load.start()
    left = ((1.0 - keep_rate) * ortho_ref[...]).astype(BF16)
    for t in range(tiles):
        for load in loads[t][:2]:
            load.wait()
        place(core_ref[0], count, per, own, other, hi, lo, t)
        for store in stores[t][:2]:
            store.start()
        change = nt(left, hi[t * width : (t + 1) * width, :])
        for load in loads[t][2:]:
            load.wait()
        out[t] = mom[t] + grad[t].astype(F32) - change
        stores[t][2].start()
    for group in stores:
        for store in group:
            store.wait()


def update_momentum(core, momentum, gradient, ortho, own, other):
    rows, cols = momentum.shape
    rank = own.shape[2]
    tile = (TILES, rows, cols // TILES)
    part = jax.ShapeDtypeStruct((cols, rank), BF16)
    return pl.pallas_call(
        early_kernel,
        in_specs=[IN_SMEM, HBM, HBM, IN_VMEM, HBM, HBM],
        out_specs=[HBM] * 3,
        out_shape=[jax.ShapeDtypeStruct((rows, cols), F32), part, part],
        scratch_shapes=[
            VMEM(tile, F32), VMEM(tile, BF16), VMEM(own.shape, F32), VMEM(own.shape, F32),
            VMEM(tile, F32), VMEM((cols, rank), BF16), VMEM((cols, rank), BF16),
            pltpu.SemaphoreType.DMA((TILES, 4)), pltpu.SemaphoreType.DMA((TILES, 3)),
        ],
        compiler_params=pltpu.CompilerParams(vmem_limit_bytes=53 * 2**20),
        cost_estimate=pl.CostEstimate(
            flops=2 * rows * cols * rank, bytes_accessed=rows * cols * 18, transcendentals=0
        ),
    )(core, momentum, gradient, ortho, own, other)


def late_kernel(chip_ref, weight_ref, got_ref, ortho_ref, back_ref, hi_ref, lo_ref,
                out_ref, basis_ref,
                weight, back, hi, lo, out, load_sems, store_sems, back_sem, *, scale, total_cols):
    tiles, rows, width = weight.shape
    loads, stores = [], []
    for t in range(tiles):
        cols = pl.ds(t * width, width)
        loads.append(copies_of(
            [
                (hi_ref.at[cols], hi.at[cols]), (lo_ref.at[cols], lo.at[cols]),
                (weight_ref.at[:, cols], weight.at[t]),
            ],
            load_sems.at[t],
        ))
        stores.append(pltpu.make_async_copy(out.at[t], out_ref.at[:, cols], store_sems.at[t]))
        for load in loads[t]:
            load.start()
    own = pltpu.make_async_copy(back_ref.at[chip_ref[0]], back, back_sem)
    own.start()
    sums = got_ref[0, 0:1, :]
    for i in range(1, got_ref.shape[0]):
        sums = sums + got_ref[i, 0:1, :]
    rms = jnp.sqrt(sums / total_cols + 1e-06)
    left_hi, left_lo = split(scale * ortho_ref[...] / rms)
    for t in range(tiles):
        for load in loads[t]:
            load.wait()
        right_hi = hi[t * width : (t + 1) * width, :]
        right_lo = lo[t * width : (t + 1) * width, :]
        change = nt(left_hi, right_hi) + nt(left_hi, right_lo) + nt(left_lo, right_hi)
        out[t] = (
            (1.0 - step_size * decay_rate) * weight[t].astype(F32) - change
        ).astype(BF16)
        stores[t].start()
    own.wait()
    basis_ref[...] = back[...] / rms
    for store in stores:
        store.wait()


def update_weight(chip, weight, got, ortho, back, hi, lo, scale, total_cols):
    rows, cols = weight.shape
    chunks, count, rank = back.shape
    tile = (TILES, rows, cols // TILES)
    return pl.pallas_call(
        functools.partial(late_kernel, scale=scale, total_cols=total_cols),
        in_specs=[IN_SMEM, HBM, IN_VMEM, IN_VMEM, HBM, HBM, HBM],
        out_specs=[HBM, IN_VMEM],
        out_shape=[
            jax.ShapeDtypeStruct((rows, cols), BF16), jax.ShapeDtypeStruct((count, rank), F32)
        ],
        scratch_shapes=[
            VMEM(tile, BF16), VMEM((count, rank), F32),
            VMEM((cols, rank), BF16), VMEM((cols, rank), BF16), VMEM(tile, BF16),
            pltpu.SemaphoreType.DMA((TILES, 3)), pltpu.SemaphoreType.DMA((TILES,)),
            pltpu.SemaphoreType.DMA,
        ],
        compiler_params=pltpu.CompilerParams(vmem_limit_bytes=53 * 2**20),
        cost_estimate=pl.CostEstimate(
            flops=6 * rows * cols * rank, bytes_accessed=rows * cols * 8, transcendentals=0
        ),
    )(chip, weight, got, ortho, back, hi, lo)


def copies_kernel(x_ref, out_ref, sems):
    stores = copies_of([(x_ref, out_ref.at[i]) for i in range(out_ref.shape[0])], sems)
    for store in stores:
        store.start()
    for store in stores:
        store.wait()


def copies_in_hbm(x, n):
    return pl.pallas_call(
        copies_kernel,
        in_specs=[IN_VMEM],
        out_specs=HBM,
        out_shape=jax.ShapeDtypeStruct((n,) + x.shape, x.dtype),
        scratch_shapes=[pltpu.SemaphoreType.DMA((n,))],
        compiler_params=pltpu.CompilerParams(vmem_limit_bytes=8 * 2**20),
        cost_estimate=pl.CostEstimate(flops=0, bytes_accessed=4 * n * x.size, transcendentals=0),
    )(x)


def project_kernel(left_ref, right_ref, out_ref, left, right, sems):
    steps, _, width = left.shape
    loads = []
    for t in range(steps):
        part = pl.ds(t * width, width)
        loads.append(copies_of(
            [(left_ref.at[:, part], left.at[t]), (right_ref.at[part], right.at[t])], sems.at[t]
        ))
        for load in loads[t]:
            load.start()
    total = jnp.zeros(out_ref.shape, F32)
    for t in range(steps):
        for load in loads[t]:
            load.wait()
        a_hi, a_lo = split(left[t])
        b_hi, b_lo = split(right[t])
        total = total + (nn(a_hi, b_hi) + nn(a_hi, b_lo) + nn(a_lo, b_hi))
    out_ref[...] = total


def project(left, right):
    rows, depth = left.shape
    rank = right.shape[1]
    steps = 7
    width = depth // steps
    return pl.pallas_call(
        project_kernel,
        in_specs=[HBM, HBM],
        out_specs=IN_VMEM,
        out_shape=jax.ShapeDtypeStruct((rows, rank), F32),
        scratch_shapes=[
            VMEM((steps, rows, width), F32), VMEM((steps, width, rank), F32),
            pltpu.SemaphoreType.DMA((steps, 2)),
        ],
        compiler_params=pltpu.CompilerParams(vmem_limit_bytes=53 * 2**20),
        cost_estimate=pl.CostEstimate(
            flops=6 * rows * depth * rank, bytes_accessed=8 * rows * depth, transcendentals=0
        ),
    )(left, right)


def project_back_kernel(keep_ref, recv_ref, proj_ref, other_ref, out_ref,
                        pair, out, load_sems, store_sems):
    chips, packed, rank = out_ref.shape
    tiles, rows, width = pair.shape
    share = rank // chips
    count = packed - share
    per = chips // tiles
    half = rows // 2
    loads, stores = [], []
    for t in range(tiles):
        cols, part = pl.ds(t * width, width), pl.ds(t * per, per)
        loads.append(copies_of(
            [
                (keep_ref.at[:, cols], pair.at[t, pl.ds(0, half)]),
                (recv_ref.at[:, cols], pair.at[t, pl.ds(half, half)]),
            ],
            load_sems.at[t],
        ))
        stores.append(pltpu.make_async_copy(out.at[part], out_ref.at[part], store_sems.at[t]))
        for load in loads[t]:
            load.start()
    proj = jnp.concatenate([proj_ref[...], other_ref[...]], axis=0)
    left_hi, left_lo = split(proj.T)

    def product(right):
        hi, lo = split(right)
        return nn(left_hi, hi) + nn(left_hi, lo) + nn(left_lo, hi)

    gram = product(proj)
    for i in range(chips):
        out[i, count:, :] = gram[i * share : (i + 1) * share, :]
    for t in range(tiles):
        for load in loads[t]:
            load.wait()
        raw = product(pair[t]).T
        for i in range(per):
            out[t * per + i, :count, :] = raw[i * count : (i + 1) * count, :]
        stores[t].start()
    for store in stores:
        store.wait()


def project_back(keep, recv, proj, other, chips):
    rows, cols = keep.shape
    rank = proj.shape[1]
    tiles = 2
    shape = (chips, cols // chips + rank // chips, rank)
    return pl.pallas_call(
        project_back_kernel,
        in_specs=[HBM, HBM, IN_VMEM, IN_VMEM],
        out_specs=HBM,
        out_shape=jax.ShapeDtypeStruct(shape, F32),
        scratch_shapes=[
            VMEM((tiles, 2 * rows, cols // tiles), F32), VMEM(shape, F32),
            pltpu.SemaphoreType.DMA((tiles, 2)), pltpu.SemaphoreType.DMA((tiles,)),
        ],
        compiler_params=pltpu.CompilerParams(vmem_limit_bytes=53 * 2**20),
        cost_estimate=pl.CostEstimate(
            flops=12 * rows * cols * rank, bytes_accessed=rows * cols * 8, transcendentals=0
        ),
    )(keep, recv, proj, other)


def across_cores(x):
    return lax.ppermute(x, "c", [(0, 1), (1, 0)])


def gather(x, axes, n):
    spread = jnp.broadcast_to(x[None], (n,) + x.shape)
    return lax.all_to_all(spread, axes, 0, 0)


def per_device(momentum, gradient, weight, basis):
    chips = lax.axis_size("x") * lax.axis_size("y")
    cores = lax.axis_size("c")
    depth = lax.axis_size("z")
    plane = ("x", "y")
    rows, cols = momentum.shape
    count, rank = basis.shape
    total_cols = cols * depth
    total_rows = rows * chips * cores
    core = lax.axis_index("c").astype(jnp.int32).reshape(1)

    keep, send = sort_columns(core, momentum, gradient, count)
    pieces = 4
    recv = jnp.concatenate([across_cores(piece) for piece in jnp.split(send, pieces, axis=0)])
    right = lax.all_to_all(copies_in_hbm(basis, chips), plane, 0, 0).reshape(chips * count, rank)

    theirs = across_cores(project(recv, right))
    partial = project(keep, right) + theirs
    share = rows // depth
    piece = jnp.sum(lax.all_to_all(partial.reshape(depth, share, rank), "z", 0, 0), axis=0)
    proj = gather(piece, "z", depth).reshape(rows, rank)
    proj_other = across_cores(proj)

    packed = project_back(keep, recv, proj, proj_other, chips)
    summed = jnp.sum(lax.all_to_all(packed, plane, 0, 0), axis=0)
    everything = gather(summed, plane, chips)
    back, ortho, sums = factor(everything, proj, cores * depth)
    back_other = across_cores(back)
    sums = lax.all_to_all(sums, ("c", "z"), 0, 0)
    new_momentum, hi, lo = update_momentum(core, momentum, gradient, ortho, back, back_other)
    sums, hi, lo = lax.optimization_barrier((sums, hi, lo))
    chip = (lax.axis_index("x") * lax.axis_size("y") + lax.axis_index("y")).astype(jnp.int32)
    scale = step_size * math.sqrt(total_cols / total_rows)
    new_weight, new_basis = update_weight(
        chip.reshape(1), weight, sums, ortho, back, hi, lo, scale, total_cols
    )
    return new_momentum, new_weight, new_basis


def solution(mesh):
    fsdp, depth = mesh.devices.shape
    grid = Mesh(mesh.devices.reshape(4, 4, 2, depth), ("x", "y", "c", "z"))
    block = P(("x", "y", "c"), "z")
    rows = P(("z", "x", "y", "c"), None)
    return jax.shard_map(
        per_device, mesh=grid, in_specs=(block, block, block, rows),
        out_specs=(block, block, rows), check_vma=False,
    )
```

```python
import functools
import math

import jax
import jax.numpy as jnp
from jax import lax
from jax.experimental import pallas as pl
from jax.experimental.pallas import tpu as pltpu
from jax.sharding import Mesh, PartitionSpec as P

keep_rate = 0.95
step_size = 0.25
decay_rate = 0.1

F32 = jnp.float32
BF16 = jnp.bfloat16
HIGH = lax.Precision.HIGH
HIGHEST = lax.Precision.HIGHEST
VMEM = pltpu.VMEM
TILES = 4
HBM = pl.BlockSpec(memory_space=pltpu.HBM)
IN_VMEM = pl.BlockSpec(memory_space=VMEM)
IN_SMEM = pl.BlockSpec(memory_space=pltpu.SMEM)


def split(x):
    hi = x.astype(BF16)
    lo = (x - hi.astype(F32)).astype(BF16)
    return hi, lo


def nt(a, b):
    return lax.dot_general(a, b, (((1,), (1,)), ((), ())), preferred_element_type=F32)


def nn(a, b):
    return lax.dot_general(a, b, (((1,), (0,)), ((), ())), preferred_element_type=F32)


def copies_of(pairs, sems):
    return [pltpu.make_async_copy(src, dst, sems.at[i]) for i, (src, dst) in enumerate(pairs)]


def sort_columns_kernel(core_ref, mom_ref, grad_ref, keep_ref, *rest, count):
    send_refs, (mom, grad, load_sems) = rest[:-3], rest[-3:]
    steps, tile, cols = mom.shape
    per = steps // len(send_refs)
    loads = []
    for t in range(steps):
        rows = pl.ds(t * tile, tile)
        loads.append(copies_of(
            [(mom_ref.at[rows, :], mom.at[t]), (grad_ref.at[rows, :], grad.at[t])],
            load_sems.at[t],
        ))
        for load in loads[t]:
            load.start()
    for t in range(steps):
        for load in loads[t]:
            load.wait()
        buffer = mom[t] + grad[t].astype(F32)
        parts = [
            jnp.concatenate(
                [buffer[:, i * count : (i + 1) * count] for i in range(first, cols // count, 2)],
                axis=1,
            )
            for first in range(2)
        ]
        send_ref = send_refs[t // per]
        there = slice(t % per * tile, (t % per + 1) * tile)
        here = slice(t * tile, (t + 1) * tile)

        @pl.when(core_ref[0] == 0)
        def _():
            keep_ref[here, :] = parts[0]
            send_ref[there, :] = parts[1]

        @pl.when(core_ref[0] == 1)
        def _():
            keep_ref[here, :] = parts[1]
            send_ref[there, :] = parts[0]


def sort_columns(core, momentum, gradient, count, pieces):
    rows, cols = momentum.shape
    steps = 8
    tile = rows // steps
    return pl.pallas_call(
        functools.partial(sort_columns_kernel, count=count),
        in_specs=[IN_SMEM, HBM, HBM],
        out_specs=[IN_VMEM] * (1 + pieces),
        out_shape=[jax.ShapeDtypeStruct((rows, cols // 2), F32)]
        + [jax.ShapeDtypeStruct((rows // pieces, cols // 2), F32)] * pieces,
        scratch_shapes=[
            VMEM((steps, tile, cols), F32), VMEM((steps, tile, cols), BF16),
            pltpu.SemaphoreType.DMA((steps, 2)),
        ],
        compiler_params=pltpu.CompilerParams(vmem_limit_bytes=16 * 2**20),
        cost_estimate=pl.CostEstimate(
            flops=rows * cols, bytes_accessed=rows * cols * 10, transcendentals=0
        ),
    )(core, momentum, gradient)


def bc(x):
    return jnp.broadcast_to(x, (8, 128))


def split3(x):
    hi = x.astype(BF16)
    rest = x - hi.astype(F32)
    mid = rest.astype(BF16)
    return hi, mid, (rest - mid.astype(F32)).astype(BF16)


def dot3(dims, a, b):
    a_hi, a_lo = split(a)
    b_hi, b_lo = split(b)
    dot = functools.partial(
        lax.dot_general, dimension_numbers=(dims, ((), ())), preferred_element_type=F32
    )
    return dot(a_hi, b_hi) + dot(a_hi, b_lo) + dot(a_lo, b_hi)


NT = ((1,), (1,))


def eliminate(top, below, tiles, a):
    cols = [[bc(a[i : i + 8, top + m : top + m + 1]) for m in range(8)] for i in below]
    own = [bc(a[top : top + 8, top + m : top + m + 1]) for m in range(8)]
    e = [[bc(own[j][i : i + 1, :]) if i >= j else None for j in range(8)] for i in range(8)]
    inv = [None] * 8
    for j in range(8):
        inv[j] = lax.rsqrt(e[j][j])
        for i in range(j + 1, 8):
            e[i][j] = e[i][j] * inv[j]
        for k in range(j + 1, 8):
            for i in range(k, 8):
                e[i][k] = e[i][k] - e[i][j] * e[k][j]
    xs = [[None] * 8 for _ in range(8)]
    for i in range(8):
        xs[i][i] = inv[i]
        for j in range(i):
            total = e[i][j] * xs[j][j]
            for k in range(j + 1, i):
                total = total + e[i][k] * xs[k][j]
            xs[i][j] = -total * inv[i]
    sub = lax.broadcasted_iota(jnp.int32, (8, 128), 0)
    for ref, t in tiles:
        rows = [bc(ref[top + k : top + k + 1, t : t + 128]) for k in range(8)]
        made = []
        for i in range(8):
            total = xs[i][0] * rows[0]
            for k in range(1, i + 1):
                total = total + xs[i][k] * rows[k]
            made.append(total)
        if below:
            back = []
            for m in range(8):
                total = xs[m][m] * made[m]
                for i in range(m + 1, 8):
                    total = total + xs[i][m] * made[i]
                back.append(total)
            for n_at, i in enumerate(below):
                value = ref[i : i + 8, t : t + 128]
                for m in range(8):
                    value = value - cols[n_at][m] * back[m]
                ref[i : i + 8, t : t + 128] = value
        row = made[0]
        for i in range(1, 8):
            row = jnp.where(sub == i, made[i], row)
        ref[top : top + 8, t : t + 128] = row


def factor_kernel(got_ref, proj_ref, back_ref, ortho_ref, sums_ref, a, w):
    chips, packed, n = got_ref.shape
    share = n // chips
    count = packed - share
    panel = 32
    for i in range(chips):
        a[i * share : (i + 1) * share, :] = got_ref[i, count:, :]
    w[...] = (
        lax.broadcasted_iota(jnp.int32, (n, n), 0) == lax.broadcasted_iota(jnp.int32, (n, n), 1)
    ).astype(F32)
    for r0 in range(0, n, panel):
        end = r0 + panel
        tiles = [(a, t) for t in range(r0 // 128 * 128, n, 128)]
        tiles += [(w, t) for t in range(0, end, 128)]
        for top in range(r0, end, 8):
            eliminate(top, list(range(top + 8, end, 8)), tiles, a)
        if end < n:
            lo, width = end // 128 * 128, -(-end // 128) * 128
            u = a[r0:end, lo:]
            v = jnp.concatenate([u, w[r0:end, :width]], axis=1)
            uh, um, ul = split3(u)
            vh, vm, vl = split3(v)
            change = lax.dot_general(
                jnp.concatenate([uh, uh, um, uh, ul, um], axis=0),
                jnp.concatenate([vh, vm, vh, vl, vh, vm], axis=0),
                (((0,), (0,)), ((), ())), preferred_element_type=F32,
            )
            a[end:n, lo:] -= change[end - lo :, : n - lo]
            w[end:n, :width] -= change[end - lo :, n - lo :]
    inverse = w[...]
    total = jnp.zeros((1, n), F32)
    group = 4
    for i in range(0, chips, group):
        rows = jnp.concatenate([got_ref[i + k, :count, :] for k in range(group)], axis=0)
        back = dot3(NT, rows, inverse)
        for k in range(group):
            back_ref[i + k] = back[k * count : (k + 1) * count]
        total = total + jnp.sum(back * back, axis=0, keepdims=True)
    sums_ref[...] = jnp.broadcast_to(total[None], sums_ref.shape)
    ortho_ref[...] = dot3(NT, proj_ref[...], inverse)


def factor(got, proj, copies):
    chips, packed, n = got.shape
    rows = proj.shape[0]
    return pl.pallas_call(
        factor_kernel,
        out_shape=[
            jax.ShapeDtypeStruct((chips, packed - n // chips, n), F32),
            jax.ShapeDtypeStruct((rows, n), F32),
            jax.ShapeDtypeStruct((copies, 8, n), F32),
        ],
        in_specs=[IN_VMEM] * 2,
        out_specs=[IN_VMEM] * 3,
        scratch_shapes=[VMEM((n, n), F32), VMEM((n, n), F32)],
        compiler_params=pltpu.CompilerParams(vmem_limit_bytes=16 * 2**20),
        cost_estimate=pl.CostEstimate(flops=40 * n**3, bytes_accessed=16 * n * n, transcendentals=0),
    )(got, proj)


def place(core, count, per, own, other, hi, lo, t):
    for i in range(t * per, (t + 1) * per):
        mine = pl.ds(pl.multiple_of((2 * i + core) * count, 16), count)
        theirs = pl.ds(pl.multiple_of((2 * i + 1 - core) * count, 16), count)
        for rows, value in ((mine, own[i]), (theirs, other[i])):
            hi[rows, :], lo[rows, :] = split(value)


def early_kernel(core_ref, mom_ref, grad_ref, ortho_ref, own_ref, other_ref,
                 out_ref, hi_ref, lo_ref,
                 mom, grad, own, other, out, hi, lo, load_sems, store_sems):
    tiles, rows, width = mom.shape
    chunks, count, _ = own.shape
    per = chunks // tiles
    loads, stores = [], []
    for t in range(tiles):
        cols, part = pl.ds(t * width, width), pl.ds(t * per, per)
        loads.append(copies_of(
            [
                (own_ref.at[part], own.at[part]), (other_ref.at[part], other.at[part]),
                (mom_ref.at[:, cols], mom.at[t]), (grad_ref.at[:, cols], grad.at[t]),
            ],
            load_sems.at[t],
        ))
        stores.append(copies_of(
            [
                (hi.at[cols], hi_ref.at[cols]), (lo.at[cols], lo_ref.at[cols]),
                (out.at[t], out_ref.at[:, cols]),
            ],
            store_sems.at[t],
        ))
        for load in loads[t]:
            load.start()
    left = ((1.0 - keep_rate) * ortho_ref[...]).astype(BF16)
    for t in range(tiles):
        for load in loads[t][:2]:
            load.wait()
        place(core_ref[0], count, per, own, other, hi, lo, t)
        for store in stores[t][:2]:
            store.start()
        change = nt(left, hi[t * width : (t + 1) * width, :])
        for load in loads[t][2:]:
            load.wait()
        out[t] = mom[t] + grad[t].astype(F32) - change
        stores[t][2].start()
    for group in stores:
        for store in group:
            store.wait()


def update_momentum(core, momentum, gradient, ortho, own, other):
    rows, cols = momentum.shape
    rank = own.shape[2]
    tile = (TILES, rows, cols // TILES)
    part = jax.ShapeDtypeStruct((cols, rank), BF16)
    return pl.pallas_call(
        early_kernel,
        in_specs=[IN_SMEM, HBM, HBM, IN_VMEM, HBM, HBM],
        out_specs=[HBM] * 3,
        out_shape=[jax.ShapeDtypeStruct((rows, cols), F32), part, part],
        scratch_shapes=[
            VMEM(tile, F32), VMEM(tile, BF16), VMEM(own.shape, F32), VMEM(own.shape, F32),
            VMEM(tile, F32), VMEM((cols, rank), BF16), VMEM((cols, rank), BF16),
            pltpu.SemaphoreType.DMA((TILES, 4)), pltpu.SemaphoreType.DMA((TILES, 3)),
        ],
        compiler_params=pltpu.CompilerParams(vmem_limit_bytes=53 * 2**20),
        cost_estimate=pl.CostEstimate(
            flops=2 * rows * cols * rank, bytes_accessed=rows * cols * 18, transcendentals=0
        ),
    )(core, momentum, gradient, ortho, own, other)


def late_kernel(chip_ref, weight_ref, got_ref, ortho_ref, back_ref, hi_ref, lo_ref,
                out_ref, basis_ref,
                weight, back, hi, lo, out, load_sems, store_sems, back_sem, *, scale, total_cols):
    tiles, rows, width = weight.shape
    loads, stores = [], []
    for t in range(tiles):
        cols = pl.ds(t * width, width)
        loads.append(copies_of(
            [
                (hi_ref.at[cols], hi.at[cols]), (lo_ref.at[cols], lo.at[cols]),
                (weight_ref.at[:, cols], weight.at[t]),
            ],
            load_sems.at[t],
        ))
        stores.append(pltpu.make_async_copy(out.at[t], out_ref.at[:, cols], store_sems.at[t]))
        for load in loads[t]:
            load.start()
    own = pltpu.make_async_copy(back_ref.at[chip_ref[0]], back, back_sem)
    own.start()
    sums = got_ref[0, 0:1, :]
    for i in range(1, got_ref.shape[0]):
        sums = sums + got_ref[i, 0:1, :]
    rms = jnp.sqrt(sums / total_cols + 1e-06)
    left_hi, left_lo = split(scale * ortho_ref[...] / rms)
    for t in range(tiles):
        for load in loads[t]:
            load.wait()
        right_hi = hi[t * width : (t + 1) * width, :]
        right_lo = lo[t * width : (t + 1) * width, :]
        change = nt(left_hi, right_hi) + nt(left_hi, right_lo) + nt(left_lo, right_hi)
        out[t] = (
            (1.0 - step_size * decay_rate) * weight[t].astype(F32) - change
        ).astype(BF16)
        stores[t].start()
    own.wait()
    basis_ref[...] = back[...] / rms
    for store in stores:
        store.wait()


def update_weight(chip, weight, got, ortho, back, hi, lo, scale, total_cols):
    rows, cols = weight.shape
    chunks, count, rank = back.shape
    tile = (TILES, rows, cols // TILES)
    return pl.pallas_call(
        functools.partial(late_kernel, scale=scale, total_cols=total_cols),
        in_specs=[IN_SMEM, HBM, IN_VMEM, IN_VMEM, HBM, HBM, HBM],
        out_specs=[HBM, IN_VMEM],
        out_shape=[
            jax.ShapeDtypeStruct((rows, cols), BF16), jax.ShapeDtypeStruct((count, rank), F32)
        ],
        scratch_shapes=[
            VMEM(tile, BF16), VMEM((count, rank), F32),
            VMEM((cols, rank), BF16), VMEM((cols, rank), BF16), VMEM(tile, BF16),
            pltpu.SemaphoreType.DMA((TILES, 3)), pltpu.SemaphoreType.DMA((TILES,)),
            pltpu.SemaphoreType.DMA,
        ],
        compiler_params=pltpu.CompilerParams(vmem_limit_bytes=53 * 2**20),
        cost_estimate=pl.CostEstimate(
            flops=6 * rows * cols * rank, bytes_accessed=rows * cols * 8, transcendentals=0
        ),
    )(chip, weight, got, ortho, back, hi, lo)


def project_kernel(right_ref, *refs):
    left_refs, out_ref = refs[:-1], refs[-1]
    b_hi, b_lo = split(right_ref[...])
    rows = left_refs[0].shape[0]
    for i, left_ref in enumerate(left_refs):
        a_hi, a_lo = split(left_ref[...])
        out_ref[i * rows : (i + 1) * rows, :] = nn(a_hi, b_hi) + nn(a_hi, b_lo) + nn(a_lo, b_hi)


def project(lefts, right):
    depth, rank = right.shape
    rows = sum(left.shape[0] for left in lefts)
    return pl.pallas_call(
        project_kernel,
        in_specs=[IN_VMEM] * (1 + len(lefts)),
        out_specs=IN_VMEM,
        out_shape=jax.ShapeDtypeStruct((rows, rank), F32),
        compiler_params=pltpu.CompilerParams(vmem_limit_bytes=14 * 2**20),
        cost_estimate=pl.CostEstimate(
            flops=6 * rows * depth * rank, bytes_accessed=8 * rows * depth, transcendentals=0
        ),
    )(right, *lefts)


def project_back_kernel(proj_ref, other_ref, *refs):
    left_refs, out_ref = refs[:-1], refs[-1]
    chips, packed, rank = out_ref.shape
    share = rank // chips
    count = packed - share
    proj = jnp.concatenate([proj_ref[...], other_ref[...]], axis=0)
    left_hi, left_lo = split(proj.T)
    per = 8
    width = per * count

    def product(right):
        hi, lo = split(right)
        return nn(left_hi, hi) + nn(left_hi, lo) + nn(left_lo, hi)

    gram = product(proj)
    for i in range(chips):
        out_ref[i, count:, :] = gram[i * share : (i + 1) * share, :]
    for t in range(chips // per):
        cols = slice(t * width, (t + 1) * width)
        raw = product(jnp.concatenate([ref[:, cols] for ref in left_refs], axis=0)).T
        for i in range(per):
            out_ref[t * per + i, :count, :] = raw[i * count : (i + 1) * count, :]


def project_back(lefts, proj, other, chips):
    cols = lefts[0].shape[1]
    rows, rank = proj.shape
    return pl.pallas_call(
        project_back_kernel,
        in_specs=[IN_VMEM] * (2 + len(lefts)),
        out_specs=IN_VMEM,
        out_shape=jax.ShapeDtypeStruct((chips, cols // chips + rank // chips, rank), F32),
        compiler_params=pltpu.CompilerParams(vmem_limit_bytes=24 * 2**20),
        cost_estimate=pl.CostEstimate(
            flops=12 * rows * cols * rank, bytes_accessed=rows * cols * 8, transcendentals=0
        ),
    )(proj, other, *lefts)


def across_cores(x):
    return lax.ppermute(x, "c", [(0, 1), (1, 0)])


def gather(x, axes, n):
    spread = jnp.broadcast_to(x[None], (n,) + x.shape)
    return lax.all_to_all(spread, axes, 0, 0)


def per_device(momentum, gradient, weight, basis):
    chips = lax.axis_size("x") * lax.axis_size("y")
    cores = lax.axis_size("c")
    depth = lax.axis_size("z")
    plane = ("x", "y")
    rows, cols = momentum.shape
    count, rank = basis.shape
    total_cols = cols * depth
    total_rows = rows * chips * cores
    core = lax.axis_index("c").astype(jnp.int32).reshape(1)

    keep, *send = sort_columns(core, momentum, gradient, count, 4)
    recv = [across_cores(piece) for piece in send]
    right = gather(basis, plane, chips).reshape(chips * count, rank)

    theirs = across_cores(project(recv, right))
    partial = project([keep], right) + theirs
    share = rows // depth
    piece = jnp.sum(lax.all_to_all(partial.reshape(depth, share, rank), "z", 0, 0), axis=0)
    proj = gather(piece, "z", depth).reshape(rows, rank)
    proj_other = across_cores(proj)

    packed = project_back([keep] + recv, proj, proj_other, chips)
    summed = jnp.sum(lax.all_to_all(packed, plane, 0, 0), axis=0)
    everything = gather(summed, plane, chips)
    back, ortho, sums = factor(everything, proj, cores * depth)
    back_other = across_cores(back)
    sums = lax.all_to_all(sums, ("c", "z"), 0, 0)
    new_momentum, hi, lo = update_momentum(core, momentum, gradient, ortho, back, back_other)
    sums, hi, lo = lax.optimization_barrier((sums, hi, lo))
    chip = (lax.axis_index("x") * lax.axis_size("y") + lax.axis_index("y")).astype(jnp.int32)
    scale = step_size * math.sqrt(total_cols / total_rows)
    new_weight, new_basis = update_weight(
        chip.reshape(1), weight, sums, ortho, back, hi, lo, scale, total_cols
    )
    return new_momentum, new_weight, new_basis


def solution(mesh):
    fsdp, depth = mesh.devices.shape
    grid = Mesh(mesh.devices.reshape(4, 4, 2, depth), ("x", "y", "c", "z"))
    block = P(("x", "y", "c"), "z")
    rows = P(("z", "x", "y", "c"), None)
    return jax.shard_map(
        per_device, mesh=grid, in_specs=(block, block, block, rows),
        out_specs=(block, block, rows), check_vma=False,
    )
```

```python
import functools
import math

import jax
import jax.numpy as jnp
from jax import lax
from jax.experimental import pallas as pl
from jax.experimental.pallas import tpu as pltpu
from jax.sharding import Mesh, PartitionSpec as P

keep_rate = 0.95
step_size = 0.25
decay_rate = 0.1

F32 = jnp.float32
BF16 = jnp.bfloat16
HIGH = lax.Precision.HIGH
HIGHEST = lax.Precision.HIGHEST
VMEM = pltpu.VMEM
TILES = 4
HBM = pl.BlockSpec(memory_space=pltpu.HBM)
IN_VMEM = pl.BlockSpec(memory_space=VMEM)
IN_SMEM = pl.BlockSpec(memory_space=pltpu.SMEM)


def split(x):
    hi = x.astype(BF16)
    lo = (x - hi.astype(F32)).astype(BF16)
    return hi, lo


def nt(a, b):
    return lax.dot_general(a, b, (((1,), (1,)), ((), ())), preferred_element_type=F32)


def nn(a, b):
    return lax.dot_general(a, b, (((1,), (0,)), ((), ())), preferred_element_type=F32)


def copies_of(pairs, sems):
    return [pltpu.make_async_copy(src, dst, sems.at[i]) for i, (src, dst) in enumerate(pairs)]


def sort_columns_kernel(core_ref, mom_ref, grad_ref, keep_ref, *rest, count):
    send_refs, (mom, grad, load_sems) = rest[:-3], rest[-3:]
    steps, tile, cols = mom.shape
    per = steps // len(send_refs)
    loads = []
    for t in range(steps):
        rows = pl.ds(t * tile, tile)
        loads.append(copies_of(
            [(mom_ref.at[rows, :], mom.at[t]), (grad_ref.at[rows, :], grad.at[t])],
            load_sems.at[t],
        ))
        for load in loads[t]:
            load.start()
    for t in range(steps):
        for load in loads[t]:
            load.wait()
        buffer = mom[t] + grad[t].astype(F32)
        parts = [
            jnp.concatenate(
                [buffer[:, i * count : (i + 1) * count] for i in range(first, cols // count, 2)],
                axis=1,
            )
            for first in range(2)
        ]
        send_ref = send_refs[t // per]
        there = slice(t % per * tile, (t % per + 1) * tile)
        here = slice(t * tile, (t + 1) * tile)

        @pl.when(core_ref[0] == 0)
        def _():
            keep_ref[here, :] = parts[0]
            send_ref[there, :] = parts[1]

        @pl.when(core_ref[0] == 1)
        def _():
            keep_ref[here, :] = parts[1]
            send_ref[there, :] = parts[0]


def sort_columns(core, momentum, gradient, count, pieces):
    rows, cols = momentum.shape
    steps = 8
    tile = rows // steps
    return pl.pallas_call(
        functools.partial(sort_columns_kernel, count=count),
        in_specs=[IN_SMEM, HBM, HBM],
        out_specs=[IN_VMEM] * (1 + pieces),
        out_shape=[jax.ShapeDtypeStruct((rows, cols // 2), F32)]
        + [jax.ShapeDtypeStruct((rows // pieces, cols // 2), F32)] * pieces,
        scratch_shapes=[
            VMEM((steps, tile, cols), F32), VMEM((steps, tile, cols), BF16),
            pltpu.SemaphoreType.DMA((steps, 2)),
        ],
        compiler_params=pltpu.CompilerParams(vmem_limit_bytes=16 * 2**20),
        cost_estimate=pl.CostEstimate(
            flops=rows * cols, bytes_accessed=rows * cols * 10, transcendentals=0
        ),
    )(core, momentum, gradient)


def bc(x):
    return jnp.broadcast_to(x, (8, 128))


def split3(x):
    hi = x.astype(BF16)
    rest = x - hi.astype(F32)
    mid = rest.astype(BF16)
    return hi, mid, (rest - mid.astype(F32)).astype(BF16)


def dot3(dims, a, b):
    a_hi, a_lo = split(a)
    b_hi, b_lo = split(b)
    dot = functools.partial(
        lax.dot_general, dimension_numbers=(dims, ((), ())), preferred_element_type=F32
    )
    return dot(a_hi, b_hi) + dot(a_hi, b_lo) + dot(a_lo, b_hi)


NT = ((1,), (1,))


def eliminate(top, below, tiles, a):
    cols = [[bc(a[i : i + 8, top + m : top + m + 1]) for m in range(8)] for i in below]
    own = [bc(a[top : top + 8, top + m : top + m + 1]) for m in range(8)]
    e = [[bc(own[j][i : i + 1, :]) if i >= j else None for j in range(8)] for i in range(8)]
    inv = [None] * 8
    for j in range(8):
        inv[j] = lax.rsqrt(e[j][j])
        for i in range(j + 1, 8):
            e[i][j] = e[i][j] * inv[j]
        for k in range(j + 1, 8):
            for i in range(k, 8):
                e[i][k] = e[i][k] - e[i][j] * e[k][j]
    xs = [[None] * 8 for _ in range(8)]
    for i in range(8):
        xs[i][i] = inv[i]
        for j in range(i):
            total = e[i][j] * xs[j][j]
            for k in range(j + 1, i):
                total = total + e[i][k] * xs[k][j]
            xs[i][j] = -total * inv[i]
    sub = lax.broadcasted_iota(jnp.int32, (8, 128), 0)
    for ref, t in tiles:
        rows = [bc(ref[top + k : top + k + 1, t : t + 128]) for k in range(8)]
        made = []
        for i in range(8):
            total = xs[i][0] * rows[0]
            for k in range(1, i + 1):
                total = total + xs[i][k] * rows[k]
            made.append(total)
        if below:
            back = []
            for m in range(8):
                total = xs[m][m] * made[m]
                for i in range(m + 1, 8):
                    total = total + xs[i][m] * made[i]
                back.append(total)
            for n_at, i in enumerate(below):
                value = ref[i : i + 8, t : t + 128]
                for m in range(8):
                    value = value - cols[n_at][m] * back[m]
                ref[i : i + 8, t : t + 128] = value
        row = made[0]
        for i in range(1, 8):
            row = jnp.where(sub == i, made[i], row)
        ref[top : top + 8, t : t + 128] = row


def factor_kernel(got_ref, proj_ref, back_ref, ortho_ref, sums_ref, a, w):
    chips, packed, n = got_ref.shape
    share = n // chips
    count = packed - share
    panel = 32
    for i in range(chips):
        a[i * share : (i + 1) * share, :] = got_ref[i, count:, :]
    w[...] = (
        lax.broadcasted_iota(jnp.int32, (n, n), 0) == lax.broadcasted_iota(jnp.int32, (n, n), 1)
    ).astype(F32)
    for r0 in range(0, n, panel):
        end = r0 + panel
        tiles = [(a, t) for t in range(r0 // 128 * 128, n, 128)]
        tiles += [(w, t) for t in range(0, end, 128)]
        for top in range(r0, end, 8):
            eliminate(top, list(range(top + 8, end, 8)), tiles, a)
        if end < n:
            lo, width = end // 128 * 128, -(-end // 128) * 128
            u = a[r0:end, lo:]
            v = jnp.concatenate([u, w[r0:end, :width]], axis=1)
            uh, um, ul = split3(u)
            vh, vm, vl = split3(v)
            change = lax.dot_general(
                jnp.concatenate([uh, uh, um, uh, ul, um], axis=0),
                jnp.concatenate([vh, vm, vh, vl, vh, vm], axis=0),
                (((0,), (0,)), ((), ())), preferred_element_type=F32,
            )
            a[end:n, lo:] -= change[end - lo :, : n - lo]
            w[end:n, :width] -= change[end - lo :, n - lo :]
    inverse = w[...]
    total = jnp.zeros((1, n), F32)
    group = 4
    for i in range(0, chips, group):
        rows = jnp.concatenate([got_ref[i + k, :count, :] for k in range(group)], axis=0)
        back = dot3(NT, rows, inverse)
        for k in range(group):
            back_ref[i + k] = back[k * count : (k + 1) * count]
        total = total + jnp.sum(back * back, axis=0, keepdims=True)
    sums_ref[...] = jnp.broadcast_to(total[None], sums_ref.shape)
    ortho_ref[...] = dot3(NT, proj_ref[...], inverse)


def factor(got, proj, copies):
    chips, packed, n = got.shape
    rows = proj.shape[0]
    return pl.pallas_call(
        factor_kernel,
        out_shape=[
            jax.ShapeDtypeStruct((chips, packed - n // chips, n), F32),
            jax.ShapeDtypeStruct((rows, n), F32),
            jax.ShapeDtypeStruct((copies, 8, n), F32),
        ],
        in_specs=[IN_VMEM] * 2,
        out_specs=[IN_VMEM] * 3,
        scratch_shapes=[VMEM((n, n), F32), VMEM((n, n), F32)],
        compiler_params=pltpu.CompilerParams(vmem_limit_bytes=16 * 2**20),
        cost_estimate=pl.CostEstimate(flops=40 * n**3, bytes_accessed=16 * n * n, transcendentals=0),
    )(got, proj)


def place(core, count, per, own, other, hi, lo, t):
    for i in range(t * per, (t + 1) * per):
        mine = pl.ds(pl.multiple_of((2 * i + core) * count, 16), count)
        theirs = pl.ds(pl.multiple_of((2 * i + 1 - core) * count, 16), count)
        for rows, value in ((mine, own[i]), (theirs, other[i])):
            hi[rows, :], lo[rows, :] = split(value)


def early_kernel(core_ref, mom_ref, grad_ref, ortho_ref, own_ref, other_ref,
                 out_ref, hi_ref, lo_ref,
                 mom, grad, own, other, out, hi, lo, load_sems, store_sems):
    tiles, rows, width = mom.shape
    chunks, count, _ = own.shape
    per = chunks // tiles
    loads, stores = [], []
    for t in range(tiles):
        cols, part = pl.ds(t * width, width), pl.ds(t * per, per)
        loads.append(copies_of(
            [
                (own_ref.at[part], own.at[part]), (other_ref.at[part], other.at[part]),
                (mom_ref.at[:, cols], mom.at[t]), (grad_ref.at[:, cols], grad.at[t]),
            ],
            load_sems.at[t],
        ))
        stores.append(copies_of(
            [
                (hi.at[cols], hi_ref.at[cols]), (lo.at[cols], lo_ref.at[cols]),
                (out.at[t], out_ref.at[:, cols]),
            ],
            store_sems.at[t],
        ))
        for load in loads[t]:
            load.start()
    left = ((1.0 - keep_rate) * ortho_ref[...]).astype(BF16)
    for t in range(tiles):
        for load in loads[t][:2]:
            load.wait()
        place(core_ref[0], count, per, own, other, hi, lo, t)
        for store in stores[t][:2]:
            store.start()
        change = nt(left, hi[t * width : (t + 1) * width, :])
        for load in loads[t][2:]:
            load.wait()
        out[t] = mom[t] + grad[t].astype(F32) - change
        stores[t][2].start()
    for group in stores:
        for store in group:
            store.wait()


def update_momentum(core, momentum, gradient, ortho, own, other):
    rows, cols = momentum.shape
    rank = own.shape[2]
    tile = (TILES, rows, cols // TILES)
    part = jax.ShapeDtypeStruct((cols, rank), BF16)
    return pl.pallas_call(
        early_kernel,
        in_specs=[IN_SMEM, HBM, HBM, IN_VMEM, HBM, HBM],
        out_specs=[HBM] * 3,
        out_shape=[jax.ShapeDtypeStruct((rows, cols), F32), part, part],
        scratch_shapes=[
            VMEM(tile, F32), VMEM(tile, BF16), VMEM(own.shape, F32), VMEM(own.shape, F32),
            VMEM(tile, F32), VMEM((cols, rank), BF16), VMEM((cols, rank), BF16),
            pltpu.SemaphoreType.DMA((TILES, 4)), pltpu.SemaphoreType.DMA((TILES, 3)),
        ],
        compiler_params=pltpu.CompilerParams(vmem_limit_bytes=53 * 2**20),
        cost_estimate=pl.CostEstimate(
            flops=2 * rows * cols * rank, bytes_accessed=rows * cols * 18, transcendentals=0
        ),
    )(core, momentum, gradient, ortho, own, other)


def late_kernel(chip_ref, weight_ref, got_ref, ortho_ref, back_ref, hi_ref, lo_ref,
                out_ref, basis_ref,
                weight, back, hi, lo, out, load_sems, store_sems, back_sem, *, scale, total_cols):
    tiles, rows, width = weight.shape
    loads, stores = [], []
    for t in range(tiles):
        cols = pl.ds(t * width, width)
        loads.append(copies_of(
            [
                (hi_ref.at[cols], hi.at[cols]), (lo_ref.at[cols], lo.at[cols]),
                (weight_ref.at[:, cols], weight.at[t]),
            ],
            load_sems.at[t],
        ))
        stores.append(pltpu.make_async_copy(out.at[t], out_ref.at[:, cols], store_sems.at[t]))
        for load in loads[t]:
            load.start()
    own = pltpu.make_async_copy(back_ref.at[chip_ref[0]], back, back_sem)
    own.start()
    sums = got_ref[0, 0:1, :]
    for i in range(1, got_ref.shape[0]):
        sums = sums + got_ref[i, 0:1, :]
    rms = jnp.sqrt(sums / total_cols + 1e-06)
    left_hi, left_lo = split(scale * ortho_ref[...] / rms)
    for t in range(tiles):
        for load in loads[t]:
            load.wait()
        right_hi = hi[t * width : (t + 1) * width, :]
        right_lo = lo[t * width : (t + 1) * width, :]
        change = nt(left_hi, right_hi) + nt(left_hi, right_lo) + nt(left_lo, right_hi)
        out[t] = (
            (1.0 - step_size * decay_rate) * weight[t].astype(F32) - change
        ).astype(BF16)
        stores[t].start()
    own.wait()
    basis_ref[...] = back[...] / rms
    for store in stores:
        store.wait()


def update_weight(chip, weight, got, ortho, back, hi, lo, scale, total_cols):
    rows, cols = weight.shape
    chunks, count, rank = back.shape
    tile = (TILES, rows, cols // TILES)
    return pl.pallas_call(
        functools.partial(late_kernel, scale=scale, total_cols=total_cols),
        in_specs=[IN_SMEM, HBM, IN_VMEM, IN_VMEM, HBM, HBM, HBM],
        out_specs=[HBM, IN_VMEM],
        out_shape=[
            jax.ShapeDtypeStruct((rows, cols), BF16), jax.ShapeDtypeStruct((count, rank), F32)
        ],
        scratch_shapes=[
            VMEM(tile, BF16), VMEM((count, rank), F32),
            VMEM((cols, rank), BF16), VMEM((cols, rank), BF16), VMEM(tile, BF16),
            pltpu.SemaphoreType.DMA((TILES, 3)), pltpu.SemaphoreType.DMA((TILES,)),
            pltpu.SemaphoreType.DMA,
        ],
        compiler_params=pltpu.CompilerParams(vmem_limit_bytes=53 * 2**20),
        cost_estimate=pl.CostEstimate(
            flops=6 * rows * cols * rank, bytes_accessed=rows * cols * 8, transcendentals=0
        ),
    )(chip, weight, got, ortho, back, hi, lo)


def project_kernel(right_ref, *refs):
    left_refs, out_ref = refs[:-1], refs[-1]
    b_hi, b_lo = split(right_ref[...])
    left = jnp.concatenate([left_ref[...] for left_ref in left_refs], axis=0)
    a_hi, a_lo = split(left)
    out_ref[...] = nn(a_hi, b_hi) + nn(a_hi, b_lo) + nn(a_lo, b_hi)


def project(lefts, right):
    depth, rank = right.shape
    rows = sum(left.shape[0] for left in lefts)
    return pl.pallas_call(
        project_kernel,
        in_specs=[IN_VMEM] * (1 + len(lefts)),
        out_specs=IN_VMEM,
        out_shape=jax.ShapeDtypeStruct((rows, rank), F32),
        compiler_params=pltpu.CompilerParams(vmem_limit_bytes=14 * 2**20),
        cost_estimate=pl.CostEstimate(
            flops=6 * rows * depth * rank, bytes_accessed=8 * rows * depth, transcendentals=0
        ),
    )(right, *lefts)


def project_back_kernel(proj_ref, other_ref, *refs):
    left_refs, out_ref = refs[:-1], refs[-1]
    chips, packed, rank = out_ref.shape
    share = rank // chips
    count = packed - share
    proj = jnp.concatenate([proj_ref[...], other_ref[...]], axis=0)
    left_hi, left_lo = split(proj.T)
    per = 8
    width = per * count

    def product(right):
        hi, lo = split(right)
        return nn(left_hi, hi) + nn(left_hi, lo) + nn(left_lo, hi)

    gram = product(proj)
    for i in range(chips):
        out_ref[i, count:, :] = gram[i * share : (i + 1) * share, :]
    for t in range(chips // per):
        cols = slice(t * width, (t + 1) * width)
        raw = product(jnp.concatenate([ref[:, cols] for ref in left_refs], axis=0)).T
        for i in range(per):
            out_ref[t * per + i, :count, :] = raw[i * count : (i + 1) * count, :]


def project_back(lefts, proj, other, chips):
    cols = lefts[0].shape[1]
    rows, rank = proj.shape
    return pl.pallas_call(
        project_back_kernel,
        in_specs=[IN_VMEM] * (2 + len(lefts)),
        out_specs=IN_VMEM,
        out_shape=jax.ShapeDtypeStruct((chips, cols // chips + rank // chips, rank), F32),
        compiler_params=pltpu.CompilerParams(vmem_limit_bytes=24 * 2**20),
        cost_estimate=pl.CostEstimate(
            flops=12 * rows * cols * rank, bytes_accessed=rows * cols * 8, transcendentals=0
        ),
    )(proj, other, *lefts)


def across_cores(x):
    return lax.ppermute(x, "c", [(0, 1), (1, 0)])


def gather(x, axes, n):
    spread = jnp.broadcast_to(x[None], (n,) + x.shape)
    return lax.all_to_all(spread, axes, 0, 0)


def per_device(momentum, gradient, weight, basis):
    chips = lax.axis_size("x") * lax.axis_size("y")
    cores = lax.axis_size("c")
    depth = lax.axis_size("z")
    plane = ("x", "y")
    rows, cols = momentum.shape
    count, rank = basis.shape
    total_cols = cols * depth
    total_rows = rows * chips * cores
    core = lax.axis_index("c").astype(jnp.int32).reshape(1)

    keep, *send = sort_columns(core, momentum, gradient, count, 4)
    recv = [across_cores(piece) for piece in send]
    right = gather(basis, plane, chips).reshape(chips * count, rank)

    theirs = across_cores(project(recv, right))
    partial = project([keep], right) + theirs
    share = rows // depth
    piece = jnp.sum(lax.all_to_all(partial.reshape(depth, share, rank), "z", 0, 0), axis=0)
    proj = gather(piece, "z", depth).reshape(rows, rank)
    proj_other = across_cores(proj)

    packed = project_back([keep] + recv, proj, proj_other, chips)
    summed = jnp.sum(lax.all_to_all(packed, plane, 0, 0), axis=0)
    everything = gather(summed, plane, chips)
    back, ortho, sums = factor(everything, proj, cores * depth)
    back_other = across_cores(back)
    sums = lax.all_to_all(sums, ("c", "z"), 0, 0)
    new_momentum, hi, lo = update_momentum(core, momentum, gradient, ortho, back, back_other)
    sums, hi, lo = lax.optimization_barrier((sums, hi, lo))
    chip = (lax.axis_index("x") * lax.axis_size("y") + lax.axis_index("y")).astype(jnp.int32)
    scale = step_size * math.sqrt(total_cols / total_rows)
    new_weight, new_basis = update_weight(
        chip.reshape(1), weight, sums, ortho, back, hi, lo, scale, total_cols
    )
    return new_momentum, new_weight, new_basis


def solution(mesh):
    fsdp, depth = mesh.devices.shape
    grid = Mesh(mesh.devices.reshape(4, 4, 2, depth), ("x", "y", "c", "z"))
    block = P(("x", "y", "c"), "z")
    rows = P(("z", "x", "y", "c"), None)
    return jax.shard_map(
        per_device, mesh=grid, in_specs=(block, block, block, rows),
        out_specs=(block, block, rows), check_vma=False,
    )
```
